32 devices in a mesh: group: 4 (over y, core), node: 2 (over x), gpu: 4 (over z).
Axes of the slice: x: 2, y: 2, z: 4, core: 2. Of those that a mesh axis runs over, the one named last changes fastest.
Arguments:
- tokens: bfloat16 [4096, 12288], P(('group', 'node', 'gpu')), may hold values from -6 to 6
- weight: bfloat16 [12288, 256], P(('node', 'gpu')), may hold values from -0.0546875 to 0.0546875
- grad_out: bfloat16 [4096, 256], P(('group', 'node', 'gpu')), may hold values from -0.25 to 0.25
Outputs:
- output: bfloat16 [4096, 256], P(('group', 'node', 'gpu'))
- weight_grad: float32 [12288, 256], P(('node', 'gpu'))
The draws below stay inside these ranges and needn't reach their ends.
All inputs are finite; a program needn't handle non-finite values.
Results may differ from the reference program's by a relative error of at most 0.0029.
Values may be sent and summed in bfloat16 or wider, within the bound.
A program may use at most 128 MiB of HBM per device.

```python
import jax
import jax.numpy as jnp
from jax import lax

D = 12288
COLS = 256
TOK_DEV = 128
TOKENS = 4096


def spiked(result, own_key, source, target, blocks, factor):
    def block_of(dim):
        return (jnp.arange(result.shape[dim]) // (result.shape[dim] // blocks)).reshape((-1,) + (1,) * (result.ndim - 1 - dim))

    near = jax.random.permutation(own_key, blocks)[block_of(target)]
    far = (block_of(target) + blocks // 2) % blocks
    return jnp.where((block_of(source) == near) | (block_of(source) == far), factor * result, result)


def block_levels(key, shape, shards, least, top_value):
    def one(axis_at, shards_of):
        heights = jax.random.uniform(jax.random.fold_in(jax.random.fold_in(key, 6), axis_at), (shards_of,), jnp.float32, least / len(shards), top_value / len(shards))
        return jnp.repeat(jnp.exp(heights), shape[axis_at] // shards_of).reshape((-1,) + (1,) * (len(shape) - axis_at - 1))

    loudness = one(*shards[0])
    for cut in shards[1:]:
        loudness = loudness * one(*cut)
    return loudness


def centred(stream_key, shape, width, limit, shards=(), kind=jnp.bfloat16):
    result = jax.random.normal(stream_key, shape, jnp.float32) * width
    if len(shards) > 0:
        result = block_levels(stream_key, shape, shards, -0.22, 0.18) * result
    return jnp.clip(result, min=-limit, max=limit).astype(kind)


def gaussian_with(stream_key, extent, width, bound, split, heavy, held_as=jnp.bfloat16):
    drawn = width * jax.random.normal(stream_key, extent, jnp.float32)
    if split:
        drawn = drawn * block_levels(stream_key, extent, split, -0.22, 0.18)
    return jnp.clip(spiked(drawn, jax.random.fold_in(stream_key, 3), *heavy), -bound, bound).astype(held_as)


def setup_inputs(seed: int = 0) -> dict:
    seeds = jax.random.split(jax.random.key(seed), 4)
    return {
        "tokens": gaussian_with(seeds[0], (TOKENS, D), 1.0, 6.0, ((0, 32),), (0, 1, 32, 2.75)),
        "weight": centred(seeds[1], (D, COLS), D ** -0.5, 0.0546875, ((0, 8),)),
        "grad_out": centred(seeds[2], (TOKENS, COLS), (TOKENS ** -0.5), 0.25, ((0, 32),)),
    }


def reference(tokens, weight, grad_out):
    output = jnp.dot(tokens, weight, preferred_element_type=jnp.float32).astype(jnp.bfloat16)
    count_blocks = tokens.shape[0] // TOK_DEV
    token_blocks = tokens.reshape(count_blocks, TOK_DEV, D)
    grad_blocks = grad_out.reshape(count_blocks, TOK_DEV, COLS)

    def accumulate(running, block_pair):
        local_term = jnp.dot(block_pair[0].T, block_pair[1], preferred_element_type=jnp.float32)
        rounded = lax.optimization_barrier(local_term.astype(jnp.bfloat16))
        return running + rounded.astype(jnp.float32), None

    weight_grad, unused = lax.scan(accumulate, jnp.zeros((D, COLS), jnp.float32), (token_blocks, grad_blocks))
    return output, weight_grad
```

```python
import functools

import jax
import jax.numpy as jnp
from jax import lax
from jax.experimental import pallas as pl
from jax.experimental.pallas import tpu as pltpu
from jax.sharding import PartitionSpec as P

MESH = pl.DeviceIdType.MESH
BF16, F32 = jnp.bfloat16, jnp.float32


def kernel(Y, N, Z, K, tok, wgt, gout, out, wgrad, T, G, W, SX, RX, SZ, RZ, SY, RY, F, acc, PO, OB,
           tl, ts, tr, gl, gs, gr, wl, wr, zs, xs, ys, sx, rx, sz, rz, sy, ry, fl, fs, fr, ps, pr, ol):
    g, n, z = lax.axis_index("group"), lax.axis_index("node"), lax.axis_index("gpu")
    y, c = g // 2, g % 2
    O = N * Z
    B = tok.shape[0]
    H = T.shape[2]
    C = H // K
    Q = H // Y
    mate = (y * 2 + 1 - c, n, z)

    def xdev(e):
        return (g, lax.rem(n + e, N), z)

    def zdev(d):
        return (g, n, lax.rem(z + d, Z))

    def ydev(f):
        return (lax.rem(y + f, Y) * 2 + c, n, z)

    def own(e, d):
        return lax.rem(n + e, N) * Z + lax.rem(z + d, Z)

    def back(e, d):
        return lax.rem(n + N - e, N) * Z + lax.rem(z + Z - d, Z)

    def remote(src, dst, send, recv, dev):
        return pltpu.make_async_remote_copy(src_ref=src, dst_ref=dst, send_sem=send, recv_sem=recv,
                                            device_id=dev, device_id_type=MESH)

    mine = pl.ds(pl.multiple_of(c * B, B), B)
    order = [(e, d) for e in list(range(1, N)) + [0] for d in list(range(1, Z)) + [0]]
    pending = []

    def cols(o, half):
        return pl.ds(pl.multiple_of(o * 2 * H + half * H, 128), H)

    glocal = pltpu.make_async_copy(gout, G.at[mine, :], gl)
    glocal.start()
    tlocal = {}
    for e, d in order:
        o = own(e, d)
        tlocal[e, d] = pltpu.make_async_copy(tok.at[:, cols(o, c)], T.at[o, mine, :], tl.at[o])
        tlocal[e, d].start()
    me = own(0, 0)
    wlocal = pltpu.make_async_copy(wgt.at[pl.ds(pl.multiple_of(c * H, H), H), :], W.at[me], wl)
    wlocal.start()

    peers = [mate] + [xdev(e) for e in range(1, N)] + [zdev(d) for d in range(1, Z)] + [ydev(f) for f in range(1, Y)]
    barrier = pltpu.get_barrier_semaphore()
    for p in peers:
        pl.semaphore_signal(barrier, inc=1, device_id=p, device_id_type=MESH)
    pl.semaphore_wait(barrier, len(peers))

    gsend = remote(gout, G.at[mine, :], gs, gr, mate)
    gsend.start()
    tsend = {}
    for e, d in order:
        o = own(e, d)
        tsend[e, d] = remote(tok.at[:, cols(o, 1 - c)], T.at[o, mine, :], ts.at[o], tr.at[o], mate)
        tsend[e, d].start()

    def part(o, q):
        return W.at[o, pl.ds(pl.multiple_of(q * Q, Q), Q), :]

    wown = wgt.at[pl.ds(pl.multiple_of(c * H + y * Q, Q), Q), :]
    for d in range(1, Z):
        s = remote(wown, part(me, y), zs.at[d], wr.at[me, y], zdev(d))
        s.start()
        pending.append(s)
    for e in range(1, N):
        s = remote(wown, part(me, y), xs.at[e, 0], wr.at[me, y], xdev(e))
        s.start()
        pending.append(s)

    def arrived(o, q):
        remote(part(o, q), part(o, q), zs.at[0], wr.at[o, q], mate).wait_recv()

    def spread(o, slot):
        for f in range(1, Y):
            s = remote(part(o, y), part(o, y), ys.at[f, slot], wr.at[o, y], ydev(f))
            s.start()
            pending.append(s)

    def from_z(d):
        o = back(0, d)
        arrived(o, y)
        for e in range(1, N):
            s = remote(part(o, y), part(o, y), xs.at[e, d], wr.at[o, y], xdev(e))
            s.start()
            pending.append(s)
        spread(o, d)

    def from_x(e, d):
        o = back(e, d)
        arrived(o, y)
        spread(o, e * Z + d)

    events = [functools.partial(from_z, d) for d in range(1, Z)]
    events += [functools.partial(from_x, e, d) for e in range(1, N) for d in range(Z)]

    def rows(k):
        return pl.ds(k * C, C)

    def ready(e, d):
        tlocal[e, d].wait()
        tsend[e, d].wait_recv()

    def term(o, k):
        total = None
        for b in range(2):
            t = lax.dot_general(T[o, pl.ds(b * B, B), rows(k)], G[pl.ds(b * B, B), :],
                                (((0,), (0,)), ((), ())), preferred_element_type=F32)
            t = t.astype(BF16).astype(F32)
            total = t if total is None else total + t
        return total

    glocal.wait()
    gsend.wait_recv()
    xsend = {}
    for e in range(1, N):
        for d in list(range(1, Z)) + [0]:
            ready(e, d)
            for k in range(K):
                SX[e - 1, d, rows(k), :] = term(own(e, d), k).astype(BF16)
                s = remote(SX.at[e - 1, d, rows(k), :], RX.at[e - 1, d, rows(k), :],
                           sx.at[e - 1, d, k], rx.at[e - 1, d, k], xdev(e))
                s.start()
                xsend[e, d, k] = s
    zsend = {}
    for d in list(range(1, Z)) + [0]:
        ready(0, d)
        for k in range(K):
            total = term(own(0, d), k)
            for e in range(1, N):
                xsend[e, d, k].wait_recv()
                total = total + RX[e - 1, d, rows(k), :].astype(F32)
            if d:
                SZ[d - 1, rows(k), :] = total.astype(BF16)
                s = remote(SZ.at[d - 1, rows(k), :], RZ.at[d - 1, rows(k), :],
                           sz.at[d - 1, k], rz.at[d - 1, k], zdev(d))
                s.start()
                zsend[d, k] = s
            else:
                SY[rows(k), :] = total
            if events:
                events.pop(0)()
    for event in events:
        event()

    ysend = {}
    for k in range(K):
        total = SY[rows(k), :]
        for d in range(1, Z):
            zsend[d, k].wait_recv()
            total = total + RZ[d - 1, rows(k), :].astype(F32)
        SY[rows(k), :] = total
        for f in range(1, Y):
            s = remote(SY.at[rows(k), :], RY.at[f - 1, rows(k), :], sy.at[f - 1, k], ry.at[f - 1, k], ydev(f))
            s.start()
            ysend[f, k] = s

    wlocal.wait()
    acc[...] = jnp.dot(T[me], W[me], preferred_element_type=F32)
    for e in range(N):
        for d in range(Z):
            if e or d:
                o = back(e, d)
                for f in range(1, Y):
                    arrived(o, lax.rem(y + f, Y))
                acc[...] += jnp.dot(T[o], W[o], preferred_element_type=F32)
    theirs = pl.ds(pl.multiple_of((1 - c) * B, B), B)
    psend = remote(acc.at[theirs, :], PO, ps, pr, mate)
    psend.start()

    fsend = []
    for k in range(K):
        total = SY[rows(k), :]
        if Y == 2:
            ysend[1, k].wait_recv()
            total = total + RY[0, rows(k), :]
        elif Y > 2:
            for f in range(1, Y):
                ysend[f, k].wait_recv()
            total = jnp.zeros((C, total.shape[1]), F32)
            for q in range(Y):
                at = lax.rem(y - q + Y, Y)
                part_q = SY[rows(k), :]
                for f in range(1, Y):
                    part_q = jnp.where(at == f, RY[f - 1, rows(k), :], part_q)
                total = total + part_q
        F[rows(k), :] = total
        place = pl.ds(pl.multiple_of(c * H + k * C, C), C)
        a = pltpu.make_async_copy(F.at[rows(k), :], wgrad.at[place, :], fl.at[k])
        a.start()
        s = remote(F.at[rows(k), :], wgrad.at[place, :], fs.at[k], fr.at[k], mate)
        s.start()
        fsend.append((a, s))

    psend.wait_recv()
    OB[...] = (acc[mine, :] + PO[...]).astype(BF16)
    olocal = pltpu.make_async_copy(OB, out, ol)
    olocal.start()

    for s in pending + [gsend, psend] + list(tsend.values()) + list(xsend.values()) + list(zsend.values()) + list(ysend.values()):
        s.wait_send()
    for a, s in fsend:
        a.wait()
        s.wait()
    olocal.wait()


def fused(Y, N, Z, tokens, weight, grad_out):
    B, D = tokens.shape
    S, M = weight.shape
    H = S // 2
    K = 2
    O = N * Z
    DMA = pltpu.SemaphoreType.DMA
    scratch = [
        pltpu.VMEM((O, 2 * B, H), BF16),
        pltpu.VMEM((2 * B, M), BF16),
        pltpu.VMEM((O, H, M), BF16),
        pltpu.VMEM((N - 1, Z, H, M), BF16),
        pltpu.VMEM((N - 1, Z, H, M), BF16),
        pltpu.VMEM((Z - 1, H, M), BF16),
        pltpu.VMEM((Z - 1, H, M), BF16),
        pltpu.VMEM((H, M), F32),
        pltpu.VMEM((Y - 1, H, M), F32),
        pltpu.VMEM((H, M), F32),
        pltpu.VMEM((2 * B, M), F32),
        pltpu.VMEM((B, M), F32),
        pltpu.VMEM((B, M), BF16),
        DMA((O,)), DMA((O,)), DMA((O,)),
        DMA, DMA, DMA,
        DMA, DMA((O, Y)),
        DMA((Z,)), DMA((N, Z)), DMA((Y, O)),
        DMA((N - 1, Z, K)), DMA((N - 1, Z, K)),
        DMA((Z - 1, K)), DMA((Z - 1, K)),
        DMA((Y - 1, K)), DMA((Y - 1, K)),
        DMA((K,)), DMA((K,)), DMA((K,)),
        DMA, DMA, DMA,
    ]
    return pl.pallas_call(
        functools.partial(kernel, Y, N, Z, K),
        out_shape=(jax.ShapeDtypeStruct((B, M), BF16), jax.ShapeDtypeStruct((S, M), F32)),
        in_specs=[pl.BlockSpec(memory_space=pl.ANY)] * 3,
        out_specs=(pl.BlockSpec(memory_space=pl.ANY),) * 2,
        scratch_shapes=scratch,
        compiler_params=pltpu.CompilerParams(collective_id=0, has_side_effects=True, vmem_limit_bytes=48 * 2**20),
        cost_estimate=pl.CostEstimate(flops=4 * B * D * M, bytes_accessed=2 * B * D + 6 * S * M, transcendentals=0),
    )(tokens, weight, grad_out)


def plain(tokens, weight, grad_out):
    model_width = tokens.shape[1]
    out_cols = weight.shape[1]
    projected = jnp.dot(tokens, lax.all_gather(weight, ("node", "gpu"), axis=0, tiled=True), preferred_element_type=F32)
    term = lax.dot_general(tokens, grad_out, (((0,), (0,)), ((), ())), preferred_element_type=F32).astype(BF16)
    stacked = term.reshape(model_width, 1, out_cols)
    received = lax.all_to_all(stacked, ("node", "gpu"), split_axis=0, concat_axis=1, tiled=True)
    own_shard = jnp.sum(received, axis=1, dtype=F32)
    return projected.astype(BF16), lax.psum(own_shard, "group")


def solution(mesh):
    groups, N, Z = (mesh.shape[a] for a in ("group", "node", "gpu"))

    def local(tokens, weight, grad_out):
        half = weight.shape[0] // 2
        if groups % 2 or groups < 4 or N < 2 or Z < 2 or half % 256 or tokens.shape[0] % 128:
            return plain(tokens, weight, grad_out)
        return fused(groups // 2, N, Z, tokens, weight, grad_out)

    rows = P(("group", "node", "gpu"), None)
    owners = P(("node", "gpu"), None)
    return jax.shard_map(local, mesh=mesh, in_specs=(rows, owners, rows), out_specs=(rows, owners), check_vma=False)
```

```python
import functools

import jax
import jax.numpy as jnp
from jax import lax
from jax.experimental import pallas as pl
from jax.experimental.pallas import tpu as pltpu
from jax.sharding import PartitionSpec as P

MESH = pl.DeviceIdType.MESH
BF16, F32 = jnp.bfloat16, jnp.float32


def kernel(Y, N, Z, R, L, tok, wgt, gout, out, wgrad, T, G, W, SY, RY, OWN, SZ, RZ, QF, FIN, acc, PO, XS, XR, OB,
           tl, ts, tr, gl, gs, gr, wl, wr, zs, ys, sy, ry, sz, rz, fl, fy, fyr, fm, fmr, ps, pr, qs, qr, ol):
    g, n, z = lax.axis_index("group"), lax.axis_index("node"), lax.axis_index("gpu")
    y, c = g // 2, g % 2
    B = tok.shape[0]
    M = gout.shape[1]
    C = Y * L
    mate = (y * 2 + 1 - c, n, z)
    dorder = list(range(1, Z)) + [0]

    def xdev(e, j):
        core = c if j == 0 else 1 - c
        return (y * 2 + core, lax.rem(n + e, N), z)

    def zdev(d):
        return (g, n, lax.rem(z + d, Z))

    def ydev(f):
        return (lax.rem(y + f, Y) * 2 + c, n, z)

    def yat(f):
        return lax.rem(y + f, Y)

    def remote(src, dst, send, recv, dev):
        return pltpu.make_async_remote_copy(src_ref=src, dst_ref=dst, send_sem=send, recv_sem=recv,
                                            device_id=dev, device_id_type=MESH)

    def block(node, core):
        return pl.ds(pl.multiple_of((node * 2 + core) * B, B), B)

    mine = block(n, c)
    pending = []
    relations = [(e, j) for e in list(range(1, N)) + [0] for j in range(2) if e or j]

    def cols(d, r, e, core):
        o = lax.rem(n + e, N) * Z + lax.rem(z + d, Z)
        return pl.ds(pl.multiple_of(o * (2 * C * R) + r * 2 * C + core * C, 128), C)

    glocal = pltpu.make_async_copy(gout, G.at[mine, :], gl)
    glocal.start()
    tlocal, tsend = {}, {}
    for r in range(R):
        for d in dorder:
            tlocal[r, d] = pltpu.make_async_copy(tok.at[:, cols(d, r, 0, c)], T.at[d, mine, pl.ds(r * C, C)], tl.at[r, d])
            tlocal[r, d].start()
    wlocal = pltpu.make_async_copy(wgt.at[:, pl.ds(c * Y, Y)], W.at[z], wl)
    wlocal.start()

    peers = [xdev(e, j) for e, j in relations] + [zdev(d) for d in range(1, Z)] + [ydev(f) for f in range(1, Y)]
    barrier = pltpu.get_barrier_semaphore()
    for p in peers:
        pl.semaphore_signal(barrier, inc=1, device_id=p, device_id_type=MESH)
    pl.semaphore_wait(barrier, len(peers))

    gsend = {}
    for e, j in relations:
        gsend[e, j] = remote(gout, G.at[mine, :], gs.at[e, j], gr.at[e, j], xdev(e, j))
        gsend[e, j].start()

    def send_tokens(r, d):
        for e, j in relations:
            core = c if j == 0 else 1 - c
            s = remote(tok.at[:, cols(d, r, e, core)], T.at[d, mine, pl.ds(r * C, C)],
                       ts.at[r, d, e, j], tr.at[r, d, e, j], xdev(e, j))
            s.start()
            tsend[r, d, e, j] = s

    for d in dorder:
        send_tokens(0, d)

    for d in range(1, Z):
        s = remote(wgt.at[:, c * Y + y], W.at[z, :, y], zs.at[d], wr.at[z, y], zdev(d))
        s.start()
        pending.append(s)

    def arrived(o, q):
        remote(W.at[o, :, q], W.at[o, :, q], zs.at[0], wr.at[o, q], mate).wait_recv()

    def from_z(d):
        o = lax.rem(z + Z - d, Z)
        arrived(o, y)
        for f in range(1, Y):
            s = remote(W.at[o, :, y], W.at[o, :, y], ys.at[f, d], wr.at[o, y], ydev(f))
            s.start()
            pending.append(s)

    def term(r, d, q):
        total = None
        for b in range(2 * N):
            t = lax.dot_general(T[d, pl.ds(b * B, B), pl.ds(pl.multiple_of(r * C + q * L, 128), L)], G[pl.ds(b * B, B), :],
                                (((0,), (0,)), ((), ())), preferred_element_type=F32)
            t = t.astype(BF16).astype(F32)
            total = t if total is None else total + t
        return total

    ysend, zsend = {}, {}

    def terms(r, d):
        tlocal[r, d].wait()
        for e, j in relations:
            tsend[r, d, e, j].wait_recv()
        if r + 1 < R:
            send_tokens(r + 1, d)
        for f in range(1, Y):
            SY[r, d, f - 1] = term(r, d, yat(f)).astype(BF16)
            s = remote(SY.at[r, d, f - 1], RY.at[r, d, f - 1], sy.at[r, d, f - 1], ry.at[r, d, f - 1], ydev(f))
            s.start()
            ysend[r, d, f] = s
        OWN[r, d] = term(r, d, y)

    def ysum(r, d):
        total = OWN[r, d]
        for f in range(1, Y):
            ysend[r, d, f].wait_recv()
            total = total + RY[r, d, f - 1].astype(F32)
        if d:
            SZ[r, d - 1] = total.astype(BF16)
            s = remote(SZ.at[r, d - 1], RZ.at[r, d - 1], sz.at[r, d - 1], rz.at[r, d - 1], zdev(d))
            s.start()
            zsend[r, d] = s
        else:
            QF[r] = total

    finals = []
    ysent = {}

    def final(r):
        total = QF[r]
        for d in range(1, Z):
            zsend[r, d].wait_recv()
            total = total + RZ[r, d - 1].astype(F32)
        FIN[r] = total
        place = wgrad.at[r, c * Y + y]
        for f in range(1, Y):
            s = remote(FIN.at[r], place, fy.at[r, f - 1], fyr.at[r, f - 1], ydev(f))
            s.start()
            ysent[r, f] = s
        s = remote(FIN.at[r], place, fm.at[r, 0], fmr.at[r, 0], mate)
        s.start()
        finals.append(s)
        a = pltpu.make_async_copy(FIN.at[r], place, fl.at[r])
        a.start()
        locals_.append(a)

    locals_ = []

    def hand_on(r):
        for f in range(1, Y):
            ysent[r, f].wait_recv()
            place = wgrad.at[r, c * Y + lax.rem(y + Y - f, Y)]
            s = remote(place, place, fm.at[r, f], fmr.at[r, f], mate)
            s.start()
            finals.append(s)

    def project(d, first):
        o = lax.rem(z + d, Z)
        if d:
            for f in range(1, Y):
                arrived(o, yat(f))
        else:
            wlocal.wait()
        w = W[o].reshape(R * C, M)
        p = jnp.dot(T[d], w, preferred_element_type=F32)
        if first:
            acc[...] = p
        else:
            acc[...] += p

    glocal.wait()
    for e, j in relations:
        gsend[e, j].wait_recv()
    steps = [(r, d) for r in range(R) for d in dorder]
    at_step = {}
    for i, d in enumerate(range(1, Z)):
        at_step.setdefault(min(Z - 1 + i, (R - 1) * Z - 1), []).append(functools.partial(from_z, d))
    for r in range(R - 1):
        at_step.setdefault((r + 1) * Z + min(2, Z - 1), []).append(functools.partial(final, r))
        if r + 2 < R:
            at_step.setdefault((r + 2) * Z, []).append(functools.partial(hand_on, r))
    for i, (r, d) in enumerate(steps):
        terms(r, d)
        if i:
            ysum(*steps[i - 1])
        for event in at_step.get(i, []):
            event()
        if r == R - 1:
            project(d, d == dorder[0])
    psend = []
    for i in range(N):
        s = remote(acc.at[block(i, 1 - c), :], PO.at[i], ps.at[i], pr.at[i], mate)
        s.start()
        psend.append(s)
    ysum(*steps[-1])
    for s in psend:
        s.wait_recv()
    qsend = []
    for e in range(1, N):
        to = lax.rem(n + e, N)
        XS[e - 1] = acc[block(to, c), :] + PO[to]
        s = remote(XS.at[e - 1], XR.at[e - 1], qs.at[e - 1], qr.at[e - 1], xdev(e, 0))
        s.start()
        qsend.append(s)
    final(R - 1)
    if R > 1:
        hand_on(R - 2)
    total = acc[mine, :] + PO[n]
    for e in range(1, N):
        qsend[e - 1].wait_recv()
        total = total + XR[e - 1]
    OB[...] = total.astype(BF16)
    olocal = pltpu.make_async_copy(OB, out, ol)
    olocal.start()
    hand_on(R - 1)

    for s in pending + psend + qsend + [s for group in (gsend, tsend, ysend, zsend, ysent) for s in group.values()]:
        s.wait_send()
    for s in finals:
        s.wait()
    for a in locals_:
        a.wait()
    olocal.wait()


def fused(Y, N, Z, tokens, weight, grad_out):
    B, D = tokens.shape
    S, M = weight.shape
    L = 128
    R = S // (2 * Y * L)
    C = Y * L
    DMA = pltpu.SemaphoreType.DMA
    scratch = [
        pltpu.VMEM((Z, 2 * N * B, R * C), BF16),
        pltpu.VMEM((2 * N * B, M), BF16),
        pltpu.VMEM((Z, R, Y, L, M), BF16),
        pltpu.VMEM((R, Z, Y - 1, L, M), BF16),
        pltpu.VMEM((R, Z, Y - 1, L, M), BF16),
        pltpu.VMEM((R, Z, L, M), F32),
        pltpu.VMEM((R, Z - 1, L, M), BF16),
        pltpu.VMEM((R, Z - 1, L, M), BF16),
        pltpu.VMEM((R, L, M), F32),
        pltpu.VMEM((R, L, M), F32),
        pltpu.VMEM((2 * N * B, M), F32),
        pltpu.VMEM((N, B, M), F32),
        pltpu.VMEM((N - 1, B, M), F32),
        pltpu.VMEM((N - 1, B, M), F32),
        pltpu.VMEM((B, M), BF16),
        DMA((R, Z)), DMA((R, Z, N, 2)), DMA((R, Z, N, 2)),
        DMA, DMA((N, 2)), DMA((N, 2)),
        DMA, DMA((Z, Y)), DMA((Z,)), DMA((Y, Z)),
        DMA((R, Z, Y - 1)), DMA((R, Z, Y - 1)),
        DMA((R, Z - 1)), DMA((R, Z - 1)),
        DMA((R,)), DMA((R, Y - 1)), DMA((R, Y - 1)), DMA((R, Y)), DMA((R, Y)),
        DMA((N,)), DMA((N,)), DMA((N - 1,)), DMA((N - 1,)), DMA,
    ]
    output, grad = pl.pallas_call(
        functools.partial(kernel, Y, N, Z, R, L),
        out_shape=(jax.ShapeDtypeStruct((B, M), BF16), jax.ShapeDtypeStruct((R, 2 * Y, L, M), F32)),
        in_specs=[pl.BlockSpec(memory_space=pl.ANY)] * 3,
        out_specs=(pl.BlockSpec(memory_space=pl.ANY),) * 2,
        scratch_shapes=scratch,
        compiler_params=pltpu.CompilerParams(collective_id=0, has_side_effects=True, vmem_limit_bytes=61 * 2**20),
        cost_estimate=pl.CostEstimate(flops=4 * B * D * M, bytes_accessed=2 * B * D + 6 * S * M, transcendentals=0),
    )(tokens, weight.reshape(R, 2 * Y, L, M), grad_out)
    return output, grad.reshape(S, M)


def plain(tokens, weight, grad_out):
    model_width = tokens.shape[1]
    out_cols = weight.shape[1]
    projected = jnp.dot(tokens, lax.all_gather(weight, ("node", "gpu"), axis=0, tiled=True), preferred_element_type=F32)
    term = lax.dot_general(tokens, grad_out, (((0,), (0,)), ((), ())), preferred_element_type=F32).astype(BF16)
    stacked = term.reshape(model_width, 1, out_cols)
    received = lax.all_to_all(stacked, ("node", "gpu"), split_axis=0, concat_axis=1, tiled=True)
    own_shard = jnp.sum(received, axis=1, dtype=F32)
    return projected.astype(BF16), lax.psum(own_shard, "group")


def solution(mesh):
    groups, N, Z = (mesh.shape[a] for a in ("group", "node", "gpu"))

    def local(tokens, weight, grad_out):
        if groups % 2 or groups < 4 or N < 2 or Z < 2 or weight.shape[0] % (groups * 128) or tokens.shape[0] % 128:
            return plain(tokens, weight, grad_out)
        return fused(groups // 2, N, Z, tokens, weight, grad_out)

    rows = P(("group", "node", "gpu"), None)
    owners = P(("node", "gpu"), None)
    return jax.shard_map(local, mesh=mesh, in_specs=(rows, owners, rows), out_specs=(rows, owners), check_vma=False)
```

```python
import functools

import jax
import jax.numpy as jnp
from jax import lax
from jax.experimental import pallas as pl
from jax.experimental.pallas import tpu as pltpu
from jax.sharding import PartitionSpec as P

MESH = pl.DeviceIdType.MESH
BF16, F32 = jnp.bfloat16, jnp.float32


def kernel(Y, N, Z, R, L, AHEAD, tok, wgt, gout, out, wgrad, T, G, GT, PT, W, SY, RY, OWN, SZ, RZ, QF, FIN, acc, PO, XS, XR, OB,
           tl, ts, tr, gl, gs, gr, wl, wr, zs, ys, sy, ry, sz, rz, fl, fy, fyr, fm, fmr, ps, pr, qs, qr, ol):
    g, n, z = lax.axis_index("group"), lax.axis_index("node"), lax.axis_index("gpu")
    y, c = g // 2, g % 2
    B = tok.shape[0]
    M = gout.shape[1]
    C = Y * L
    mate = (y * 2 + 1 - c, n, z)
    dorder = list(range(1, Z)) + [0]

    def xdev(e, j):
        core = c if j == 0 else 1 - c
        return (y * 2 + core, lax.rem(n + e, N), z)

    def zdev(d):
        return (g, n, lax.rem(z + d, Z))

    def ydev(f):
        return (lax.rem(y + f, Y) * 2 + c, n, z)

    def yat(f):
        return lax.rem(y + f, Y)

    def remote(src, dst, send, recv, dev):
        return pltpu.make_async_remote_copy(src_ref=src, dst_ref=dst, send_sem=send, recv_sem=recv,
                                            device_id=dev, device_id_type=MESH)

    def block(node, core):
        return pl.ds(pl.multiple_of((node * 2 + core) * B, B), B)

    mine = block(n, c)
    pending = []
    relations = [(e, j) for e in list(range(1, N)) + [0] for j in range(2) if e or j]

    def cols(d, r, e, core):
        o = lax.rem(n + e, N) * Z + lax.rem(z + d, Z)
        return pl.ds(pl.multiple_of(o * (2 * C * R) + r * 2 * C + core * C, 128), C)

    glocal = pltpu.make_async_copy(gout, G.at[mine, :], gl)
    glocal.start()
    tlocal, tsend = {}, {}
    for r in range(R):
        for d in dorder:
            tlocal[r, d] = pltpu.make_async_copy(tok.at[:, cols(d, r, 0, c)], T.at[d, mine, pl.ds(r * C, C)], tl.at[r, d])
            tlocal[r, d].start()
    wlocal = pltpu.make_async_copy(wgt.at[:, pl.ds(c * Y, Y)], W.at[z], wl)
    wlocal.start()

    peers = [xdev(e, j) for e, j in relations] + [zdev(d) for d in range(1, Z)] + [ydev(f) for f in range(1, Y)]
    barrier = pltpu.get_barrier_semaphore()
    for p in peers:
        pl.semaphore_signal(barrier, inc=1, device_id=p, device_id_type=MESH)
    pl.semaphore_wait(barrier, len(peers))

    gsend = {}
    for e, j in relations:
        gsend[e, j] = remote(gout, G.at[mine, :], gs.at[e, j], gr.at[e, j], xdev(e, j))
        gsend[e, j].start()

    def send_tokens(r, d):
        for e, j in relations:
            core = c if j == 0 else 1 - c
            s = remote(tok.at[:, cols(d, r, e, core)], T.at[d, mine, pl.ds(r * C, C)],
                       ts.at[r, d, e, j], tr.at[r, d, e, j], xdev(e, j))
            s.start()
            tsend[r, d, e, j] = s

    steps = [(r, d) for r in range(R) for d in dorder]
    for r, d in steps[:AHEAD]:
        send_tokens(r, d)

    for d in range(1, Z):
        s = remote(wgt.at[:, c * Y + y], W.at[z, :, y], zs.at[d], wr.at[z, y], zdev(d))
        s.start()
        pending.append(s)

    def arrived(o, q):
        remote(W.at[o, :, q], W.at[o, :, q], zs.at[0], wr.at[o, q], mate).wait_recv()

    def from_z(d):
        o = lax.rem(z + Z - d, Z)
        arrived(o, y)
        for f in range(1, Y):
            s = remote(W.at[o, :, y], W.at[o, :, y], ys.at[f, d], wr.at[o, y], ydev(f))
            s.start()
            pending.append(s)

    ysend, zsend = {}, {}

    def ypart(q):
        return PT[:, pl.ds(pl.multiple_of(q * L, 128), L)]

    def terms(i, r, d):
        tlocal[r, d].wait()
        for e, j in relations:
            tsend[r, d, e, j].wait_recv()
        if i + AHEAD < len(steps):
            send_tokens(*steps[i + AHEAD])
        total = None
        for b in range(2 * N):
            t = jnp.dot(GT[:, pl.ds(b * B, B)], T[d, pl.ds(b * B, B), pl.ds(r * C, C)], preferred_element_type=F32)
            t = t.astype(BF16).astype(F32)
            total = t if total is None else total + t
        PT[...] = total
        for f in range(1, Y):
            SY[r, d, f - 1] = ypart(yat(f)).astype(BF16)
            s = remote(SY.at[r, d, f - 1], RY.at[r, d, f - 1], sy.at[r, d, f - 1], ry.at[r, d, f - 1], ydev(f))
            s.start()
            ysend[r, d, f] = s
        OWN[r, d] = ypart(y)

    def ysum(r, d):
        total = OWN[r, d]
        for f in range(1, Y):
            ysend[r, d, f].wait_recv()
            total = total + RY[r, d, f - 1].astype(F32)
        if d:
            SZ[r, d - 1] = total.astype(BF16)
            s = remote(SZ.at[r, d - 1], RZ.at[r, d - 1], sz.at[r, d - 1], rz.at[r, d - 1], zdev(d))
            s.start()
            zsend[r, d] = s
        else:
            QF[r] = total

    finals = []
    ysent = {}

    def final(r):
        total = QF[r]
        for d in range(1, Z):
            zsend[r, d].wait_recv()
            total = total + RZ[r, d - 1].astype(F32)
        FIN[r] = total.T
        place = wgrad.at[r, c * Y + y]
        for f in range(1, Y):
            s = remote(FIN.at[r], place, fy.at[r, f - 1], fyr.at[r, f - 1], ydev(f))
            s.start()
            ysent[r, f] = s
        s = remote(FIN.at[r], place, fm.at[r, 0], fmr.at[r, 0], mate)
        s.start()
        finals.append(s)
        a = pltpu.make_async_copy(FIN.at[r], place, fl.at[r])
        a.start()
        locals_.append(a)

    locals_ = []

    def hand_on(r):
        for f in range(1, Y):
            ysent[r, f].wait_recv()
            place = wgrad.at[r, c * Y + lax.rem(y + Y - f, Y)]
            s = remote(place, place, fm.at[r, f], fmr.at[r, f], mate)
            s.start()
            finals.append(s)

    def project(d, lo, hi, first):
        o = lax.rem(z + d, Z)
        w = W[o, lo:hi].reshape((hi - lo) * C, M)
        p = jnp.dot(T[d, :, lo * C:hi * C], w, preferred_element_type=F32)
        if first:
            acc[...] = p
        else:
            acc[...] += p

    def weights(d):
        if d:
            for f in range(1, Y):
                arrived(lax.rem(z + d, Z), yat(f))
        else:
            wlocal.wait()

    glocal.wait()
    for e, j in relations:
        gsend[e, j].wait_recv()
    GT[...] = G[...].astype(F32).T.astype(BF16)
    at_step = {}
    for i, d in enumerate(range(1, Z)):
        at_step.setdefault(min(Z - 1 + i, (R - 1) * Z - 1), []).append(functools.partial(from_z, d))
    for r in range(R - 1):
        at_step.setdefault((r + 1) * Z + min(2, Z - 1), []).append(functools.partial(final, r))
        if r + 2 < R:
            at_step.setdefault((r + 2) * Z, []).append(functools.partial(hand_on, r))
    for i, (r, d) in enumerate(steps):
        terms(i, r, d)
        if i:
            ysum(*steps[i - 1])
        for event in at_step.get(i, []):
            event()
        if r == R - 1:
            weights(d)
            if R > 1:
                project(d, 0, R - 1, d == dorder[0])
    ysum(*steps[-1])
    for d in dorder:
        project(d, R - 1, R, R == 1 and d == dorder[0])
    psend = []
    for i in range(N):
        s = remote(acc.at[block(i, 1 - c), :], PO.at[i], ps.at[i], pr.at[i], mate)
        s.start()
        psend.append(s)
    for s in psend:
        s.wait_recv()
    qsend = []
    for e in range(1, N):
        to = lax.rem(n + e, N)
        XS[e - 1] = acc[block(to, c), :] + PO[to]
        s = remote(XS.at[e - 1], XR.at[e - 1], qs.at[e - 1], qr.at[e - 1], xdev(e, 0))
        s.start()
        qsend.append(s)
    final(R - 1)
    if R > 1:
        hand_on(R - 2)
    total = acc[mine, :] + PO[n]
    for e in range(1, N):
        qsend[e - 1].wait_recv()
        total = total + XR[e - 1]
    OB[...] = total.astype(BF16)
    olocal = pltpu.make_async_copy(OB, out, ol)
    olocal.start()
    hand_on(R - 1)

    for s in pending + psend + qsend + [s for group in (gsend, tsend, ysend, zsend, ysent) for s in group.values()]:
        s.wait_send()
    for s in finals:
        s.wait()
    for a in locals_:
        a.wait()
    olocal.wait()


def fused(Y, N, Z, tokens, weight, grad_out):
    B, D = tokens.shape
    S, M = weight.shape
    L = 128
    R = S // (2 * Y * L)
    C = Y * L
    DMA = pltpu.SemaphoreType.DMA
    scratch = [
        pltpu.VMEM((Z, 2 * N * B, R * C), BF16),
        pltpu.VMEM((2 * N * B, M), BF16),
        pltpu.VMEM((M, 2 * N * B), BF16),
        pltpu.VMEM((M, C), F32),
        pltpu.VMEM((Z, R, Y, L, M), BF16),
        pltpu.VMEM((R, Z, Y - 1, M, L), BF16),
        pltpu.VMEM((R, Z, Y - 1, M, L), BF16),
        pltpu.VMEM((R, Z, M, L), F32),
        pltpu.VMEM((R, Z - 1, M, L), BF16),
        pltpu.VMEM((R, Z - 1, M, L), BF16),
        pltpu.VMEM((R, M, L), F32),
        pltpu.VMEM((R, L, M), F32),
        pltpu.VMEM((2 * N * B, M), F32),
        pltpu.VMEM((N, B, M), F32),
        pltpu.VMEM((N - 1, B, M), F32),
        pltpu.VMEM((N - 1, B, M), F32),
        pltpu.VMEM((B, M), BF16),
        DMA((R, Z)), DMA((R, Z, N, 2)), DMA((R, Z, N, 2)),
        DMA, DMA((N, 2)), DMA((N, 2)),
        DMA, DMA((Z, Y)), DMA((Z,)), DMA((Y, Z)),
        DMA((R, Z, Y - 1)), DMA((R, Z, Y - 1)),
        DMA((R, Z - 1)), DMA((R, Z - 1)),
        DMA((R,)), DMA((R, Y - 1)), DMA((R, Y - 1)), DMA((R, Y)), DMA((R, Y)),
        DMA((N,)), DMA((N,)), DMA((N - 1,)), DMA((N - 1,)), DMA,
    ]
    output, grad = pl.pallas_call(
        functools.partial(kernel, Y, N, Z, R, L, 2),
        out_shape=(jax.ShapeDtypeStruct((B, M), BF16), jax.ShapeDtypeStruct((R, 2 * Y, L, M), F32)),
        in_specs=[pl.BlockSpec(memory_space=pltpu.HBM)] * 3,
        out_specs=(pl.BlockSpec(memory_space=pl.ANY),) * 2,
        scratch_shapes=scratch,
        compiler_params=pltpu.CompilerParams(collective_id=0, has_side_effects=True, vmem_limit_bytes=48 * 2**20),
        cost_estimate=pl.CostEstimate(flops=4 * B * D * M, bytes_accessed=2 * B * D + 6 * S * M, transcendentals=0),
    )(*(pltpu.with_memory_space_constraint(a, pltpu.HBM) for a in (tokens, weight.reshape(R, 2 * Y, L, M), grad_out)))
    return output, grad.reshape(S, M)


def plain(tokens, weight, grad_out):
    model_width = tokens.shape[1]
    out_cols = weight.shape[1]
    projected = jnp.dot(tokens, lax.all_gather(weight, ("node", "gpu"), axis=0, tiled=True), preferred_element_type=F32)
    term = lax.dot_general(tokens, grad_out, (((0,), (0,)), ((), ())), preferred_element_type=F32).astype(BF16)
    stacked = term.reshape(model_width, 1, out_cols)
    received = lax.all_to_all(stacked, ("node", "gpu"), split_axis=0, concat_axis=1, tiled=True)
    own_shard = jnp.sum(received, axis=1, dtype=F32)
    return projected.astype(BF16), lax.psum(own_shard, "group")


def solution(mesh):
    groups, N, Z = (mesh.shape[a] for a in ("group", "node", "gpu"))

    def local(tokens, weight, grad_out):
        if groups % 2 or groups < 4 or N < 2 or Z < 2 or weight.shape[0] % (groups * 128) or tokens.shape[0] % 128:
            return plain(tokens, weight, grad_out)
        return fused(groups // 2, N, Z, tokens, weight, grad_out)

    rows = P(("group", "node", "gpu"), None)
    owners = P(("node", "gpu"), None)
    return jax.shard_map(local, mesh=mesh, in_specs=(rows, owners, rows), out_specs=(rows, owners), check_vma=False)
```

```python
import functools

import jax
import jax.numpy as jnp
from jax import lax
from jax.experimental import pallas as pl
from jax.experimental.pallas import tpu as pltpu
from jax.sharding import PartitionSpec as P

MESH = pl.DeviceIdType.MESH
BF16, F32 = jnp.bfloat16, jnp.float32


def kernel(Y, N, Z, R, L, AHEAD, tok, wgt, gout, out, wgrad, T, G, GT, PT, W, SY, RY, OWN, SZ, RZ, QF, FIN, acc, PO, XS, XR, OB,
           tl, ts, tr, gl, gs, gr, wl, wr, zs, ys, sy, ry, sz, rz, fl, fy, fyr, fm, fmr, ps, pr, qs, qr, ol):
    g, n, z = lax.axis_index("group"), lax.axis_index("node"), lax.axis_index("gpu")
    y, c = g // 2, g % 2
    B = tok.shape[0]
    M = gout.shape[1]
    C = Y * L
    mate = (y * 2 + 1 - c, n, z)
    dorder = list(range(1, Z)) + [0]

    def xdev(e, j):
        core = c if j == 0 else 1 - c
        return (y * 2 + core, lax.rem(n + e, N), z)

    def zdev(d):
        return (g, n, lax.rem(z + d, Z))

    def ydev(f):
        return (lax.rem(y + f, Y) * 2 + c, n, z)

    def yat(f):
        return lax.rem(y + f, Y)

    def remote(src, dst, send, recv, dev):
        return pltpu.make_async_remote_copy(src_ref=src, dst_ref=dst, send_sem=send, recv_sem=recv,
                                            device_id=dev, device_id_type=MESH)

    def block(node, core):
        return pl.ds(pl.multiple_of((node * 2 + core) * B, B), B)

    mine = block(n, c)
    pending = []
    relations = [(e, j) for e in list(range(1, N)) + [0] for j in range(2) if e or j]

    def cols(d, r, e, core):
        o = lax.rem(n + e, N) * Z + lax.rem(z + d, Z)
        return pl.ds(pl.multiple_of(o * (2 * C * R) + r * 2 * C + core * C, 128), C)

    glocal = pltpu.make_async_copy(gout, G.at[mine, :], gl)
    glocal.start()
    tlocal, tsend = {}, {}
    for r in range(R):
        for d in dorder:
            tlocal[r, d] = pltpu.make_async_copy(tok.at[:, cols(d, r, 0, c)], T.at[d, mine, pl.ds(r * C, C)], tl.at[r, d])
            tlocal[r, d].start()
    wlocal = pltpu.make_async_copy(wgt.at[:, pl.ds(c * Y, Y)], W.at[z], wl)
    wlocal.start()

    peers = [xdev(e, j) for e, j in relations] + [zdev(d) for d in range(1, Z)] + [ydev(f) for f in range(1, Y)]
    barrier = pltpu.get_barrier_semaphore()
    for p in peers:
        pl.semaphore_signal(barrier, inc=1, device_id=p, device_id_type=MESH)
    pl.semaphore_wait(barrier, len(peers))

    gsend = {}
    for e, j in relations:
        gsend[e, j] = remote(gout, G.at[mine, :], gs.at[e, j], gr.at[e, j], xdev(e, j))
        gsend[e, j].start()

    def send_tokens(r, d):
        for e, j in relations:
            core = c if j == 0 else 1 - c
            s = remote(tok.at[:, cols(d, r, e, core)], T.at[d, mine, pl.ds(r * C, C)],
                       ts.at[r, d, e, j], tr.at[r, d, e, j], xdev(e, j))
            s.start()
            tsend[r, d, e, j] = s

    steps = [(r, d) for r in range(R) for d in dorder]
    for r, d in steps[:AHEAD]:
        send_tokens(r, d)

    for d in range(1, Z):
        s = remote(wgt.at[:, c * Y + y], W.at[z, :, y], zs.at[d], wr.at[z, y], zdev(d))
        s.start()
        pending.append(s)

    def arrived(o, q):
        remote(W.at[o, :, q], W.at[o, :, q], zs.at[0], wr.at[o, q], mate).wait_recv()

    def from_z(d):
        o = lax.rem(z + Z - d, Z)
        arrived(o, y)
        for f in range(1, Y):
            s = remote(W.at[o, :, y], W.at[o, :, y], ys.at[f, d], wr.at[o, y], ydev(f))
            s.start()
            pending.append(s)

    ysend, zsend = {}, {}

    def ypart(q):
        return PT[:, pl.ds(pl.multiple_of(q * L, 128), L)]

    def terms(i, r, d):
        tlocal[r, d].wait()
        for e, j in relations:
            tsend[r, d, e, j].wait_recv()
        if i + AHEAD < len(steps):
            send_tokens(*steps[i + AHEAD])
        total = None
        for b in range(2 * N):
            t = jnp.dot(GT[:, pl.ds(b * B, B)], T[d, pl.ds(b * B, B), pl.ds(r * C, C)], preferred_element_type=F32)
            t = t.astype(BF16).astype(F32)
            total = t if total is None else total + t
        PT[...] = total
        for f in range(1, Y):
            SY[r, d, f - 1] = ypart(yat(f)).astype(BF16)
            s = remote(SY.at[r, d, f - 1], RY.at[r, d, f - 1], sy.at[r, d, f - 1], ry.at[r, d, f - 1], ydev(f))
            s.start()
            ysend[r, d, f] = s
        OWN[r, d] = ypart(y)

    def ysum(r, d):
        total = OWN[r, d]
        for f in range(1, Y):
            ysend[r, d, f].wait_recv()
            total = total + RY[r, d, f - 1].astype(F32)
        if d:
            SZ[r, d - 1] = total.astype(BF16)
            s = remote(SZ.at[r, d - 1], RZ.at[r, d - 1], sz.at[r, d - 1], rz.at[r, d - 1], zdev(d))
            s.start()
            zsend[r, d] = s
        else:
            QF[r] = total

    finals = []
    ysent = {}

    def final(r):
        total = QF[r]
        for d in range(1, Z):
            zsend[r, d].wait_recv()
            total = total + RZ[r, d - 1].astype(F32)
        FIN[r] = total.T
        place = wgrad.at[r, c * Y + y]
        for f in range(1, Y):
            s = remote(FIN.at[r], place, fy.at[r, f - 1], fyr.at[r, f - 1], ydev(f))
            s.start()
            ysent[r, f] = s
        s = remote(FIN.at[r], place, fm.at[r, 0], fmr.at[r, 0], mate)
        s.start()
        finals.append(s)
        a = pltpu.make_async_copy(FIN.at[r], place, fl.at[r])
        a.start()
        locals_.append(a)

    locals_ = []

    def hand_on(r):
        for f in range(1, Y):
            ysent[r, f].wait_recv()
            place = wgrad.at[r, c * Y + lax.rem(y + Y - f, Y)]
            s = remote(place, place, fm.at[r, f], fmr.at[r, f], mate)
            s.start()
            finals.append(s)

    def project(d, first):
        w = W[lax.rem(z + d, Z)].reshape(R * C, M)
        p = jnp.dot(T[d], w, preferred_element_type=F32)
        if first:
            acc[...] = p
        else:
            acc[...] += p

    def weights(d):
        if d:
            for f in range(1, Y):
                arrived(lax.rem(z + d, Z), yat(f))
        else:
            wlocal.wait()

    glocal.wait()
    for e, j in relations:
        gsend[e, j].wait_recv()
    GT[...] = G[...].astype(F32).T.astype(BF16)
    at_step = {}
    for i, d in enumerate(range(1, Z)):
        at_step.setdefault(min(Z + 1 + i, R * Z - 1), []).append(functools.partial(from_z, d))
    for r in range(R - 1):
        at_step.setdefault((r + 1) * Z + min(2, Z - 1), []).append(functools.partial(final, r))
        if r + 2 < R:
            at_step.setdefault((r + 2) * Z, []).append(functools.partial(hand_on, r))
    for i, (r, d) in enumerate(steps):
        terms(i, r, d)
        if i:
            ysum(*steps[i - 1])
        for event in at_step.get(i, []):
            event()
    ysum(*steps[-1])
    for d in [0] + list(range(1, Z)):
        weights(d)
        project(d, d == 0)
    psend = []
    for i in range(N):
        s = remote(acc.at[block(i, 1 - c), :], PO.at[i], ps.at[i], pr.at[i], mate)
        s.start()
        psend.append(s)
    for s in psend:
        s.wait_recv()
    qsend = []
    for e in range(1, N):
        to = lax.rem(n + e, N)
        XS[e - 1] = acc[block(to, c), :] + PO[to]
        s = remote(XS.at[e - 1], XR.at[e - 1], qs.at[e - 1], qr.at[e - 1], xdev(e, 0))
        s.start()
        qsend.append(s)
    final(R - 1)
    if R > 1:
        hand_on(R - 2)
    total = acc[mine, :] + PO[n]
    for e in range(1, N):
        qsend[e - 1].wait_recv()
        total = total + XR[e - 1]
    OB[...] = total.astype(BF16)
    olocal = pltpu.make_async_copy(OB, out, ol)
    olocal.start()
    hand_on(R - 1)

    for s in pending + psend + qsend + [s for group in (gsend, tsend, ysend, zsend, ysent) for s in group.values()]:
        s.wait_send()
    for s in finals:
        s.wait()
    for a in locals_:
        a.wait()
    olocal.wait()


def fused(Y, N, Z, tokens, weight, grad_out):
    B, D = tokens.shape
    S, M = weight.shape
    L = 128
    R = S // (2 * Y * L)
    C = Y * L
    DMA = pltpu.SemaphoreType.DMA
    scratch = [
        pltpu.VMEM((Z, 2 * N * B, R * C), BF16),
        pltpu.VMEM((2 * N * B, M), BF16),
        pltpu.VMEM((M, 2 * N * B), BF16),
        pltpu.VMEM((M, C), F32),
        pltpu.VMEM((Z, R, Y, L, M), BF16),
        pltpu.VMEM((R, Z, Y - 1, M, L), BF16),
        pltpu.VMEM((R, Z, Y - 1, M, L), BF16),
        pltpu.VMEM((R, Z, M, L), F32),
        pltpu.VMEM((R, Z - 1, M, L), BF16),
        pltpu.VMEM((R, Z - 1, M, L), BF16),
        pltpu.VMEM((R, M, L), F32),
        pltpu.VMEM((R, L, M), F32),
        pltpu.VMEM((2 * N * B, M), F32),
        pltpu.VMEM((N, B, M), F32),
        pltpu.VMEM((N - 1, B, M), F32),
        pltpu.VMEM((N - 1, B, M), F32),
        pltpu.VMEM((B, M), BF16),
        DMA((R, Z)), DMA((R, Z, N, 2)), DMA((R, Z, N, 2)),
        DMA, DMA((N, 2)), DMA((N, 2)),
        DMA, DMA((Z, Y)), DMA((Z,)), DMA((Y, Z)),
        DMA((R, Z, Y - 1)), DMA((R, Z, Y - 1)),
        DMA((R, Z - 1)), DMA((R, Z - 1)),
        DMA((R,)), DMA((R, Y - 1)), DMA((R, Y - 1)), DMA((R, Y)), DMA((R, Y)),
        DMA((N,)), DMA((N,)), DMA((N - 1,)), DMA((N - 1,)), DMA,
    ]
    output, grad = pl.pallas_call(
        functools.partial(kernel, Y, N, Z, R, L, 5),
        out_shape=(jax.ShapeDtypeStruct((B, M), BF16), jax.ShapeDtypeStruct((R, 2 * Y, L, M), F32)),
        in_specs=[pl.BlockSpec(memory_space=pltpu.HBM)] * 3,
        out_specs=(pl.BlockSpec(memory_space=pl.ANY),) * 2,
        scratch_shapes=scratch,
        compiler_params=pltpu.CompilerParams(collective_id=0, has_side_effects=True, vmem_limit_bytes=48 * 2**20),
        cost_estimate=pl.CostEstimate(flops=4 * B * D * M, bytes_accessed=2 * B * D + 6 * S * M, transcendentals=0),
    )(*(pltpu.with_memory_space_constraint(a, pltpu.HBM) for a in (tokens, weight.reshape(R, 2 * Y, L, M), grad_out)))
    return output, grad.reshape(S, M)


def plain(tokens, weight, grad_out):
    model_width = tokens.shape[1]
    out_cols = weight.shape[1]
    projected = jnp.dot(tokens, lax.all_gather(weight, ("node", "gpu"), axis=0, tiled=True), preferred_element_type=F32)
    term = lax.dot_general(tokens, grad_out, (((0,), (0,)), ((), ())), preferred_element_type=F32).astype(BF16)
    stacked = term.reshape(model_width, 1, out_cols)
    received = lax.all_to_all(stacked, ("node", "gpu"), split_axis=0, concat_axis=1, tiled=True)
    own_shard = jnp.sum(received, axis=1, dtype=F32)
    return projected.astype(BF16), lax.psum(own_shard, "group")


def solution(mesh):
    groups, N, Z = (mesh.shape[a] for a in ("group", "node", "gpu"))

    def local(tokens, weight, grad_out):
        if groups % 2 or groups < 4 or N < 2 or Z < 2 or weight.shape[0] % (groups * 128) or tokens.shape[0] % 128:
            return plain(tokens, weight, grad_out)
        return fused(groups // 2, N, Z, tokens, weight, grad_out)

    rows = P(("group", "node", "gpu"), None)
    owners = P(("node", "gpu"), None)
    return jax.shard_map(local, mesh=mesh, in_specs=(rows, owners, rows), out_specs=(rows, owners), check_vma=False)
```

```python
import functools

import jax
import jax.numpy as jnp
from jax import lax
from jax.experimental import pallas as pl
from jax.experimental.pallas import tpu as pltpu
from jax.sharding import PartitionSpec as P

MESH = pl.DeviceIdType.MESH
BF16, F32 = jnp.bfloat16, jnp.float32


def kernel(Y, N, Z, R, L, AHEAD, tok, wgt, gout, out, wgrad, T, XT, G, GT, PT, W, SY, RY, OWN, SZ, RZ, QF, FIN, acc, PO, XS, XR, OB,
           tl, xl, ts, tr, gl, gs, gr, wl, wr, zs, ys, sy, ry, sz, rz, fl, fy, fyr, fm, fmr, ps, pr, qs, qr, ol):
    g, n, z = lax.axis_index("group"), lax.axis_index("node"), lax.axis_index("gpu")
    y, c = g // 2, g % 2
    B = tok.shape[0]
    M = gout.shape[1]
    C = Y * L
    mate = (y * 2 + 1 - c, n, z)
    dorder = list(range(1, Z)) + [0]

    def xdev(e):
        return (g, lax.rem(n + e, N), z)

    def zdev(d):
        return (g, n, lax.rem(z + d, Z))

    def ydev(f):
        return (lax.rem(y + f, Y) * 2 + c, n, z)

    def yat(f):
        return lax.rem(y + f, Y)

    def remote(src, dst, send, recv, dev):
        return pltpu.make_async_remote_copy(src_ref=src, dst_ref=dst, send_sem=send, recv_sem=recv,
                                            device_id=dev, device_id_type=MESH)

    def block(node, core):
        return pl.ds(pl.multiple_of((node * 2 + core) * B, B), B)

    mine = block(n, c)
    pending = []

    def cols(d, r, e, core, width):
        o = lax.rem(n + e, N) * Z + lax.rem(z + d, Z)
        return pl.ds(pl.multiple_of(o * (2 * C * R) + r * 2 * C + core * C, 128), width)

    def source(e):
        return block(lax.rem(n + N - e, N), c)

    glocal = pltpu.make_async_copy(gout, G.at[mine, :], gl)
    glocal.start()
    tlocal, tsend = {}, {}
    for r in range(R):
        for d in dorder:
            tlocal[r, d] = pltpu.make_async_copy(tok.at[:, cols(d, r, 0, c, C)], T.at[d, mine, pl.ds(r * C, C)], tl.at[r, d])
            tlocal[r, d].start()
    wlocal = pltpu.make_async_copy(wgt.at[:, pl.ds(c * Y, Y)], W.at[z], wl)
    wlocal.start()

    peers = [mate] + [xdev(e) for e in range(1, N)] + [zdev(d) for d in range(1, Z)] + [ydev(f) for f in range(1, Y)]
    barrier = pltpu.get_barrier_semaphore()
    for p in peers:
        pl.semaphore_signal(barrier, inc=1, device_id=p, device_id_type=MESH)
    pl.semaphore_wait(barrier, len(peers))

    gsend = {(0, 1): remote(gout, G.at[mine, :], gs.at[0, 1], gr.at[0, 1], mate)}
    for e in range(1, N):
        gsend[e, 0] = remote(gout, G.at[mine, :], gs.at[e, 0], gr.at[e, 0], xdev(e))
    for s in gsend.values():
        s.start()

    def send_tokens(r, d):
        for e in range(1, N):
            s = remote(tok.at[:, cols(d, r, e, 0, 2 * C)], XT.at[r, d, e - 1],
                       ts.at[r, d, e, 0], tr.at[r, d, e, 0], xdev(e))
            s.start()
            tsend[r, d, e, 0] = s
        s = remote(tok.at[:, cols(d, r, 0, 1 - c, C)], T.at[d, mine, pl.ds(r * C, C)],
                   ts.at[r, d, 0, 1], tr.at[r, d, 0, 1], mate)
        s.start()
        tsend[r, d, 0, 1] = s

    xlocal = {}

    def take(i, r, d):
        def half(e, core):
            return XT.at[r, d, e - 1, :, pl.ds(pl.multiple_of(core * C, 128), C)]

        for e in range(1, N):
            tsend[r, d, e, 0].wait_recv()
            place = T.at[d, source(e), pl.ds(r * C, C)]
            s = remote(half(e, 1 - c), place, ts.at[r, d, e, 1], tr.at[r, d, e, 1], mate)
            s.start()
            tsend[r, d, e, 1] = s
            a = pltpu.make_async_copy(half(e, c), place, xl.at[r, d, e - 1])
            a.start()
            xlocal[r, d, e] = a
        if i + AHEAD < len(steps):
            send_tokens(*steps[i + AHEAD])

    steps = [(r, d) for r in range(R) for d in dorder]
    for r, d in steps[:AHEAD]:
        send_tokens(r, d)

    for d in range(1, Z):
        s = remote(wgt.at[:, c * Y + y], W.at[z, :, y], zs.at[d], wr.at[z, y], zdev(d))
        s.start()
        pending.append(s)

    def arrived(o, q):
        remote(W.at[o, :, q], W.at[o, :, q], zs.at[0], wr.at[o, q], mate).wait_recv()

    def from_z(d):
        o = lax.rem(z + Z - d, Z)
        arrived(o, y)
        for f in range(1, Y):
            s = remote(W.at[o, :, y], W.at[o, :, y], ys.at[f, d], wr.at[o, y], ydev(f))
            s.start()
            pending.append(s)

    ysend, zsend = {}, {}

    def ypart(q):
        return PT[:, pl.ds(pl.multiple_of(q * L, 128), L)]

    def terms(r, d):
        tlocal[r, d].wait()
        tsend[r, d, 0, 1].wait_recv()
        for e in range(1, N):
            xlocal[r, d, e].wait()
            tsend[r, d, e, 1].wait_recv()
        total = None
        for b in range(2 * N):
            t = jnp.dot(GT[:, pl.ds(b * B, B)], T[d, pl.ds(b * B, B), pl.ds(r * C, C)], preferred_element_type=F32)
            t = t.astype(BF16).astype(F32)
            total = t if total is None else total + t
        PT[...] = total
        for f in range(1, Y):
            SY[r, d, f - 1] = ypart(yat(f)).astype(BF16)
            s = remote(SY.at[r, d, f - 1], RY.at[r, d, f - 1], sy.at[r, d, f - 1], ry.at[r, d, f - 1], ydev(f))
            s.start()
            ysend[r, d, f] = s
        OWN[r, d] = ypart(y)

    def ysum(r, d):
        total = OWN[r, d]
        for f in range(1, Y):
            ysend[r, d, f].wait_recv()
            total = total + RY[r, d, f - 1].astype(F32)
        if d:
            SZ[r, d - 1] = total.astype(BF16)
            s = remote(SZ.at[r, d - 1], RZ.at[r, d - 1], sz.at[r, d - 1], rz.at[r, d - 1], zdev(d))
            s.start()
            zsend[r, d] = s
        else:
            QF[r] = total

    finals = []
    ysent = {}

    def final(r):
        total = QF[r]
        for d in range(1, Z):
            zsend[r, d].wait_recv()
            total = total + RZ[r, d - 1].astype(F32)
        FIN[r] = total.T
        place = wgrad.at[r, c * Y + y]
        for f in range(1, Y):
            s = remote(FIN.at[r], place, fy.at[r, f - 1], fyr.at[r, f - 1], ydev(f))
            s.start()
            ysent[r, f] = s
        s = remote(FIN.at[r], place, fm.at[r, 0], fmr.at[r, 0], mate)
        s.start()
        finals.append(s)
        a = pltpu.make_async_copy(FIN.at[r], place, fl.at[r])
        a.start()
        locals_.append(a)

    locals_ = []

    def hand_on(r):
        for f in range(1, Y):
            ysent[r, f].wait_recv()
            place = wgrad.at[r, c * Y + lax.rem(y + Y - f, Y)]
            s = remote(place, place, fm.at[r, f], fmr.at[r, f], mate)
            s.start()
            finals.append(s)

    def project(d, lo, hi, first):
        o = lax.rem(z + d, Z)
        w = W[o, lo:hi].reshape((hi - lo) * C, M)
        p = jnp.dot(T[d, :, lo * C:hi * C], w, preferred_element_type=F32)
        if first:
            acc[...] = p
        else:
            acc[...] += p

    def weights(d):
        if d:
            for f in range(1, Y):
                arrived(lax.rem(z + d, Z), yat(f))
        else:
            wlocal.wait()

    glocal.wait()
    for e in range(1, N):
        gsend[e, 0].wait_recv()
        rows = G.at[source(e), :]
        gsend[e, 1] = remote(rows, rows, gs.at[e, 1], gr.at[e, 1], mate)
        gsend[e, 1].start()
    take(0, *steps[0])
    gsend[0, 1].wait_recv()
    for e in range(1, N):
        gsend[e, 1].wait_recv()
    GT[...] = G[...].astype(F32).T.astype(BF16)
    at_step = {}
    for i, d in enumerate(range(1, Z)):
        at_step.setdefault(min(1 + i, R * Z - 1), []).append(functools.partial(from_z, d))
    for r in range(R - 1):
        at_step.setdefault((r + 1) * Z + min(2, Z - 1), []).append(functools.partial(final, r))
        if r + 2 < R:
            at_step.setdefault((r + 2) * Z, []).append(functools.partial(hand_on, r))
    for i, (r, d) in enumerate(steps):
        if i + 1 < len(steps):
            take(i + 1, *steps[i + 1])
        terms(r, d)
        if i:
            ysum(*steps[i - 1])
        for event in at_step.get(i, []):
            event()
        if r == R - 1:
            weights(d)
            if R > 1:
                project(d, 0, R - 1, d == dorder[0])
    ysum(*steps[-1])
    for d in dorder:
        project(d, R - 1, R, R == 1 and d == dorder[0])
    psend = []
    for i in range(N):
        s = remote(acc.at[block(i, 1 - c), :], PO.at[i], ps.at[i], pr.at[i], mate)
        s.start()
        psend.append(s)
    for s in psend:
        s.wait_recv()
    qsend = []
    for e in range(1, N):
        to = lax.rem(n + e, N)
        XS[e - 1] = acc[block(to, c), :] + PO[to]
        s = remote(XS.at[e - 1], XR.at[e - 1], qs.at[e - 1], qr.at[e - 1], xdev(e))
        s.start()
        qsend.append(s)
    final(R - 1)
    if R > 1:
        hand_on(R - 2)
    total = acc[mine, :] + PO[n]
    for e in range(1, N):
        qsend[e - 1].wait_recv()
        total = total + XR[e - 1]
    OB[...] = total.astype(BF16)
    olocal = pltpu.make_async_copy(OB, out, ol)
    olocal.start()
    hand_on(R - 1)

    for s in pending + psend + qsend + [s for group in (gsend, tsend, ysend, zsend, ysent) for s in group.values()]:
        s.wait_send()
    for s in finals:
        s.wait()
    for a in locals_:
        a.wait()
    olocal.wait()


def fused(Y, N, Z, tokens, weight, grad_out):
    B, D = tokens.shape
    S, M = weight.shape
    L = 128
    R = S // (2 * Y * L)
    C = Y * L
    DMA = pltpu.SemaphoreType.DMA
    scratch = [
        pltpu.VMEM((Z, 2 * N * B, R * C), BF16),
        pltpu.VMEM((R, Z, N - 1, B, 2 * C), BF16),
        pltpu.VMEM((2 * N * B, M), BF16),
        pltpu.VMEM((M, 2 * N * B), BF16),
        pltpu.VMEM((M, C), F32),
        pltpu.VMEM((Z, R, Y, L, M), BF16),
        pltpu.VMEM((R, Z, Y - 1, M, L), BF16),
        pltpu.VMEM((R, Z, Y - 1, M, L), BF16),
        pltpu.VMEM((R, Z, M, L), F32),
        pltpu.VMEM((R, Z - 1, M, L), BF16),
        pltpu.VMEM((R, Z - 1, M, L), BF16),
        pltpu.VMEM((R, M, L), F32),
        pltpu.VMEM((R, L, M), F32),
        pltpu.VMEM((2 * N * B, M), F32),
        pltpu.VMEM((N, B, M), F32),
        pltpu.VMEM((N - 1, B, M), F32),
        pltpu.VMEM((N - 1, B, M), F32),
        pltpu.VMEM((B, M), BF16),
        DMA((R, Z)), DMA((R, Z, N - 1)), DMA((R, Z, N, 2)), DMA((R, Z, N, 2)),
        DMA, DMA((N, 2)), DMA((N, 2)),
        DMA, DMA((Z, Y)), DMA((Z,)), DMA((Y, Z)),
        DMA((R, Z, Y - 1)), DMA((R, Z, Y - 1)),
        DMA((R, Z - 1)), DMA((R, Z - 1)),
        DMA((R,)), DMA((R, Y - 1)), DMA((R, Y - 1)), DMA((R, Y)), DMA((R, Y)),
        DMA((N,)), DMA((N,)), DMA((N - 1,)), DMA((N - 1,)), DMA,
    ]
    output, grad = pl.pallas_call(
        functools.partial(kernel, Y, N, Z, R, L, 3),
        out_shape=(jax.ShapeDtypeStruct((B, M), BF16), jax.ShapeDtypeStruct((R, 2 * Y, L, M), F32)),
        in_specs=[pl.BlockSpec(memory_space=pltpu.HBM)] * 3,
        out_specs=(pl.BlockSpec(memory_space=pl.ANY),) * 2,
        scratch_shapes=scratch,
        compiler_params=pltpu.CompilerParams(collective_id=0, has_side_effects=True, vmem_limit_bytes=48 * 2**20),
        cost_estimate=pl.CostEstimate(flops=4 * B * D * M, bytes_accessed=2 * B * D + 6 * S * M, transcendentals=0),
    )(*(pltpu.with_memory_space_constraint(a, pltpu.HBM) for a in (tokens, weight.reshape(R, 2 * Y, L, M), grad_out)))
    return output, grad.reshape(S, M)


def plain(tokens, weight, grad_out):
    model_width = tokens.shape[1]
    out_cols = weight.shape[1]
    projected = jnp.dot(tokens, lax.all_gather(weight, ("node", "gpu"), axis=0, tiled=True), preferred_element_type=F32)
    term = lax.dot_general(tokens, grad_out, (((0,), (0,)), ((), ())), preferred_element_type=F32).astype(BF16)
    stacked = term.reshape(model_width, 1, out_cols)
    received = lax.all_to_all(stacked, ("node", "gpu"), split_axis=0, concat_axis=1, tiled=True)
    own_shard = jnp.sum(received, axis=1, dtype=F32)
    return projected.astype(BF16), lax.psum(own_shard, "group")


def solution(mesh):
    groups, N, Z = (mesh.shape[a] for a in ("group", "node", "gpu"))

    def local(tokens, weight, grad_out):
        if groups % 2 or groups < 4 or N < 2 or Z < 2 or weight.shape[0] % (groups * 128) or tokens.shape[0] % 128:
            return plain(tokens, weight, grad_out)
        return fused(groups // 2, N, Z, tokens, weight, grad_out)

    rows = P(("group", "node", "gpu"), None)
    owners = P(("node", "gpu"), None)
    return jax.shard_map(local, mesh=mesh, in_specs=(rows, owners, rows), out_specs=(rows, owners), check_vma=False)
```

```python
import functools

import jax
import jax.numpy as jnp
from jax import lax
from jax.experimental import pallas as pl
from jax.experimental.pallas import tpu as pltpu
from jax.sharding import PartitionSpec as P

MESH = pl.DeviceIdType.MESH
BF16, F32 = jnp.bfloat16, jnp.float32


def kernel(Y, N, Z, R, L, AHEAD, tok, wgt, gout, out, wgrad, T, G, GT, PT, W, SY, RY, OWN, SZ, RZ, QF, FIN, acc, PO, XS, XR, OB,
           tl, ts, tr, gl, gs, gr, wl, wr, zs, ys, sy, ry, sz, rz, fl, fy, fyr, fm, fmr, ps, pr, qs, qr, ol):
    g, n, z = lax.axis_index("group"), lax.axis_index("node"), lax.axis_index("gpu")
    y, c = g // 2, g % 2
    B = tok.shape[0]
    M = gout.shape[1]
    C = Y * L
    mate = (y * 2 + 1 - c, n, z)
    dorder = list(range(1, Z)) + [0]

    def xdev(e, j):
        core = c if j == 0 else 1 - c
        return (y * 2 + core, lax.rem(n + e, N), z)

    def zdev(d):
        return (g, n, lax.rem(z + d, Z))

    def ydev(f):
        return (lax.rem(y + f, Y) * 2 + c, n, z)

    def yat(f):
        return lax.rem(y + f, Y)

    def remote(src, dst, send, recv, dev):
        return pltpu.make_async_remote_copy(src_ref=src, dst_ref=dst, send_sem=send, recv_sem=recv,
                                            device_id=dev, device_id_type=MESH)

    def block(node, core):
        return pl.ds(pl.multiple_of((node * 2 + core) * B, B), B)

    mine = block(n, c)
    pending = []
    relations = [(e, j) for e in list(range(1, N)) + [0] for j in range(2) if e or j]

    def cols(d, r, e, core):
        o = lax.rem(n + e, N) * Z + lax.rem(z + d, Z)
        return pl.ds(pl.multiple_of(o * (2 * C * R) + r * 2 * C + core * C, 128), C)

    glocal = pltpu.make_async_copy(gout, G.at[mine, :], gl)
    glocal.start()
    tlocal, tsend = {}, {}
    for r in range(R):
        for d in dorder:
            tlocal[r, d] = pltpu.make_async_copy(tok.at[:, cols(d, r, 0, c)], T.at[d, mine, pl.ds(r * C, C)], tl.at[r, d])
            tlocal[r, d].start()
    wlocal = pltpu.make_async_copy(wgt.at[:, pl.ds(c * Y, Y)], W.at[z], wl)
    wlocal.start()

    peers = [xdev(e, j) for e, j in relations] + [zdev(d) for d in range(1, Z)] + [ydev(f) for f in range(1, Y)]
    barrier = pltpu.get_barrier_semaphore()
    for p in peers:
        pl.semaphore_signal(barrier, inc=1, device_id=p, device_id_type=MESH)
    pl.semaphore_wait(barrier, len(peers))

    gsend = {}
    for e, j in relations:
        gsend[e, j] = remote(gout, G.at[mine, :], gs.at[e, j], gr.at[e, j], xdev(e, j))
        gsend[e, j].start()

    def send_tokens(r, d):
        for e, j in relations:
            core = c if j == 0 else 1 - c
            s = remote(tok.at[:, cols(d, r, e, core)], T.at[d, mine, pl.ds(r * C, C)],
                       ts.at[r, d, e, j], tr.at[r, d, e, j], xdev(e, j))
            s.start()
            tsend[r, d, e, j] = s

    steps = [(r, d) for r in range(R) for d in dorder]
    for r, d in steps[:AHEAD]:
        send_tokens(r, d)

    for d in range(1, Z):
        s = remote(wgt.at[:, c * Y + y], W.at[z, :, y], zs.at[d], wr.at[z, y], zdev(d))
        s.start()
        pending.append(s)

    def arrived(o, q):
        remote(W.at[o, :, q], W.at[o, :, q], zs.at[0], wr.at[o, q], mate).wait_recv()

    def from_z(d):
        o = lax.rem(z + Z - d, Z)
        arrived(o, y)
        for f in range(1, Y):
            s = remote(W.at[o, :, y], W.at[o, :, y], ys.at[f, d], wr.at[o, y], ydev(f))
            s.start()
            pending.append(s)

    ysend, zsend = {}, {}

    def ypart(q):
        return PT[:, pl.ds(pl.multiple_of(q * L, 128), L)]

    def terms(i, r, d):
        tlocal[r, d].wait()
        for e, j in relations:
            tsend[r, d, e, j].wait_recv()
        if i + AHEAD < len(steps):
            send_tokens(*steps[i + AHEAD])
        total = None
        for b in range(2 * N):
            t = jnp.dot(GT[:, pl.ds(b * B, B)], T[d, pl.ds(b * B, B), pl.ds(r * C, C)], preferred_element_type=F32)
            t = t.astype(BF16).astype(F32)
            total = t if total is None else total + t
        PT[...] = total
        for f in range(1, Y):
            SY[r, d, f - 1] = ypart(yat(f)).astype(BF16)
            s = remote(SY.at[r, d, f - 1], RY.at[r, d, f - 1], sy.at[r, d, f - 1], ry.at[r, d, f - 1], ydev(f))
            s.start()
            ysend[r, d, f] = s
        OWN[r, d] = ypart(y)

    def ysum(r, d):
        total = OWN[r, d]
        for f in range(1, Y):
            ysend[r, d, f].wait_recv()
            total = total + RY[r, d, f - 1].astype(F32)
        if d:
            SZ[r, d - 1] = total.astype(BF16)
            s = remote(SZ.at[r, d - 1], RZ.at[r, d - 1], sz.at[r, d - 1], rz.at[r, d - 1], zdev(d))
            s.start()
            zsend[r, d] = s
        else:
            QF[r] = total

    finals = []
    ysent = {}

    def final(r):
        total = QF[r]
        for d in range(1, Z):
            zsend[r, d].wait_recv()
            total = total + RZ[r, d - 1].astype(F32)
        FIN[r] = total.T
        place = wgrad.at[r, c * Y + y]
        for f in range(1, Y):
            s = remote(FIN.at[r], place, fy.at[r, f - 1], fyr.at[r, f - 1], ydev(f))
            s.start()
            ysent[r, f] = s
        s = remote(FIN.at[r], place, fm.at[r, 0], fmr.at[r, 0], mate)
        s.start()
        finals.append(s)
        a = pltpu.make_async_copy(FIN.at[r], place, fl.at[r])
        a.start()
        locals_.append(a)

    locals_ = []

    def hand_on(r):
        for f in range(1, Y):
            ysent[r, f].wait_recv()
            place = wgrad.at[r, c * Y + lax.rem(y + Y - f, Y)]
            s = remote(place, place, fm.at[r, f], fmr.at[r, f], mate)
            s.start()
            finals.append(s)

    def project(d, lo, hi, first):
        o = lax.rem(z + d, Z)
        w = W[o, lo:hi].reshape((hi - lo) * C, M)
        p = jnp.dot(T[d, :, lo * C:hi * C], w, preferred_element_type=F32)
        if first:
            acc[...] = p
        else:
            acc[...] += p

    def weights(d):
        if d:
            for f in range(1, Y):
                arrived(lax.rem(z + d, Z), yat(f))
        else:
            wlocal.wait()

    glocal.wait()
    for e, j in relations:
        gsend[e, j].wait_recv()
    GT[...] = G[...].astype(F32).T.astype(BF16)
    at_step = {}
    for i, d in enumerate(range(1, Z)):
        at_step.setdefault(min(Z - 2 + i, (R - 1) * Z - 1), []).append(functools.partial(from_z, d))
    for r in range(R - 1):
        at_step.setdefault((r + 1) * Z + min(2, Z - 1), []).append(functools.partial(final, r))
        if r + 2 < R:
            at_step.setdefault((r + 2) * Z, []).append(functools.partial(hand_on, r))
    for i, (r, d) in enumerate(steps):
        terms(i, r, d)
        if i:
            ysum(*steps[i - 1])
        for event in at_step.get(i, []):
            event()
        if r == R - 1:
            weights(d)
            if R > 1:
                project(d, 0, R - 1, d == dorder[0])
    ysum(*steps[-1])
    final(R - 1)
    if R > 1:
        hand_on(R - 2)
    for d in dorder:
        project(d, R - 1, R, R == 1 and d == dorder[0])
    psend = []
    for i in range(N):
        s = remote(acc.at[block(i, 1 - c), :], PO.at[i], ps.at[i], pr.at[i], mate)
        s.start()
        psend.append(s)
    for s in psend:
        s.wait_recv()
    qsend = []
    for e in range(1, N):
        to = lax.rem(n + e, N)
        XS[e - 1] = acc[block(to, c), :] + PO[to]
        s = remote(XS.at[e - 1], XR.at[e - 1], qs.at[e - 1], qr.at[e - 1], xdev(e, 0))
        s.start()
        qsend.append(s)
    hand_on(R - 1)
    total = acc[mine, :] + PO[n]
    for e in range(1, N):
        qsend[e - 1].wait_recv()
        total = total + XR[e - 1]
    OB[...] = total.astype(BF16)
    olocal = pltpu.make_async_copy(OB, out, ol)
    olocal.start()

    for s in pending + psend + qsend + [s for group in (gsend, tsend, ysend, zsend, ysent) for s in group.values()]:
        s.wait_send()
    for s in finals:
        s.wait()
    for a in locals_:
        a.wait()
    olocal.wait()


def fused(Y, N, Z, tokens, weight, grad_out):
    B, D = tokens.shape
    S, M = weight.shape
    L = 128
    R = S // (2 * Y * L)
    C = Y * L
    DMA = pltpu.SemaphoreType.DMA
    scratch = [
        pltpu.VMEM((Z, 2 * N * B, R * C), BF16),
        pltpu.VMEM((2 * N * B, M), BF16),
        pltpu.VMEM((M, 2 * N * B), BF16),
        pltpu.VMEM((M, C), F32),
        pltpu.VMEM((Z, R, Y, L, M), BF16),
        pltpu.VMEM((R, Z, Y - 1, M, L), BF16),
        pltpu.VMEM((R, Z, Y - 1, M, L), BF16),
        pltpu.VMEM((R, Z, M, L), F32),
        pltpu.VMEM((R, Z - 1, M, L), BF16),
        pltpu.VMEM((R, Z - 1, M, L), BF16),
        pltpu.VMEM((R, M, L), F32),
        pltpu.VMEM((R, L, M), F32),
        pltpu.VMEM((2 * N * B, M), F32),
        pltpu.VMEM((N, B, M), F32),
        pltpu.VMEM((N - 1, B, M), F32),
        pltpu.VMEM((N - 1, B, M), F32),
        pltpu.VMEM((B, M), BF16),
        DMA((R, Z)), DMA((R, Z, N, 2)), DMA((R, Z, N, 2)),
        DMA, DMA((N, 2)), DMA((N, 2)),
        DMA, DMA((Z, Y)), DMA((Z,)), DMA((Y, Z)),
        DMA((R, Z, Y - 1)), DMA((R, Z, Y - 1)),
        DMA((R, Z - 1)), DMA((R, Z - 1)),
        DMA((R,)), DMA((R, Y - 1)), DMA((R, Y - 1)), DMA((R, Y)), DMA((R, Y)),
        DMA((N,)), DMA((N,)), DMA((N - 1,)), DMA((N - 1,)), DMA,
    ]
    output, grad = pl.pallas_call(
        functools.partial(kernel, Y, N, Z, R, L, 3),
        out_shape=(jax.ShapeDtypeStruct((B, M), BF16), jax.ShapeDtypeStruct((R, 2 * Y, L, M), F32)),
        in_specs=[pl.BlockSpec(memory_space=pltpu.HBM)] * 3,
        out_specs=(pl.BlockSpec(memory_space=pl.ANY),) * 2,
        scratch_shapes=scratch,
        compiler_params=pltpu.CompilerParams(collective_id=0, has_side_effects=True, vmem_limit_bytes=48 * 2**20),
        cost_estimate=pl.CostEstimate(flops=4 * B * D * M, bytes_accessed=2 * B * D + 6 * S * M, transcendentals=0),
    )(*(pltpu.with_memory_space_constraint(a, pltpu.HBM) for a in (tokens, weight.reshape(R, 2 * Y, L, M), grad_out)))
    return output, grad.reshape(S, M)


def plain(tokens, weight, grad_out):
    model_width = tokens.shape[1]
    out_cols = weight.shape[1]
    projected = jnp.dot(tokens, lax.all_gather(weight, ("node", "gpu"), axis=0, tiled=True), preferred_element_type=F32)
    term = lax.dot_general(tokens, grad_out, (((0,), (0,)), ((), ())), preferred_element_type=F32).astype(BF16)
    stacked = term.reshape(model_width, 1, out_cols)
    received = lax.all_to_all(stacked, ("node", "gpu"), split_axis=0, concat_axis=1, tiled=True)
    own_shard = jnp.sum(received, axis=1, dtype=F32)
    return projected.astype(BF16), lax.psum(own_shard, "group")


def solution(mesh):
    groups, N, Z = (mesh.shape[a] for a in ("group", "node", "gpu"))

    def local(tokens, weight, grad_out):
        if groups % 2 or groups < 4 or N < 2 or Z < 2 or weight.shape[0] % (groups * 128) or tokens.shape[0] % 128:
            return plain(tokens, weight, grad_out)
        return fused(groups // 2, N, Z, tokens, weight, grad_out)

    rows = P(("group", "node", "gpu"), None)
    owners = P(("node", "gpu"), None)
    return jax.shard_map(local, mesh=mesh, in_specs=(rows, owners, rows), out_specs=(rows, owners), check_vma=False)
```

```python
import functools

import jax
import jax.numpy as jnp
from jax import lax
from jax.experimental import pallas as pl
from jax.experimental.pallas import tpu as pltpu
from jax.sharding import PartitionSpec as P

MESH = pl.DeviceIdType.MESH
BF16, F32 = jnp.bfloat16, jnp.float32


def kernel(Y, N, Z, R, L, AHEAD, tok, wgt, gout, out, wgrad, T, G, GT, PT, W, SY, RY, OWN, SZ, RZ, QF, FIN, acc, PO, XS, XR, OB,
           tl, ts, tr, gl, gs, gr, wl, wr, zs, ys, sy, ry, sz, rz, fl, fy, fyr, fm, fmr, ps, pr, qs, qr, ol):
    g, n, z = lax.axis_index("group"), lax.axis_index("node"), lax.axis_index("gpu")
    y, c = g // 2, g % 2
    B = tok.shape[0]
    M = gout.shape[1]
    C = Y * L
    mate = (y * 2 + 1 - c, n, z)
    dorder = list(range(1, Z)) + [0]

    def xdev(e, j):
        core = c if j == 0 else 1 - c
        return (y * 2 + core, lax.rem(n + e, N), z)

    def zdev(d):
        return (g, n, lax.rem(z + d, Z))

    def ydev(f):
        return (lax.rem(y + f, Y) * 2 + c, n, z)

    def yat(f):
        return lax.rem(y + f, Y)

    def remote(src, dst, send, recv, dev):
        return pltpu.make_async_remote_copy(src_ref=src, dst_ref=dst, send_sem=send, recv_sem=recv,
                                            device_id=dev, device_id_type=MESH)

    def block(node, core):
        return pl.ds(pl.multiple_of((node * 2 + core) * B, B), B)

    mine = block(n, c)
    pending = []
    relations = [(e, j) for e in list(range(1, N)) + [0] for j in range(2) if e or j]

    def cols(d, r, e, core):
        o = lax.rem(n + e, N) * Z + lax.rem(z + d, Z)
        return pl.ds(pl.multiple_of(o * (2 * C * R) + r * 2 * C + core * C, 128), C)

    glocal = pltpu.make_async_copy(gout, G.at[mine, :], gl)
    glocal.start()
    tlocal, tsend = {}, {}
    for r in range(R):
        for d in dorder:
            tlocal[r, d] = pltpu.make_async_copy(tok.at[:, cols(d, r, 0, c)], T.at[d, mine, pl.ds(r * C, C)], tl.at[r, d])
            tlocal[r, d].start()
    wlocal = pltpu.make_async_copy(wgt.at[:, pl.ds(c * Y, Y)], W.at[z], wl)
    wlocal.start()

    peers = [xdev(e, j) for e, j in relations] + [zdev(d) for d in range(1, Z)] + [ydev(f) for f in range(1, Y)]
    barrier = pltpu.get_barrier_semaphore()
    for p in peers:
        pl.semaphore_signal(barrier, inc=1, device_id=p, device_id_type=MESH)
    pl.semaphore_wait(barrier, len(peers))

    gsend = {}
    for e, j in relations:
        gsend[e, j] = remote(gout, G.at[mine, :], gs.at[e, j], gr.at[e, j], xdev(e, j))
        gsend[e, j].start()

    def send_tokens(r, d):
        for e, j in relations:
            core = c if j == 0 else 1 - c
            s = remote(tok.at[:, cols(d, r, e, core)], T.at[d, mine, pl.ds(r * C, C)],
                       ts.at[r, d, e, j], tr.at[r, d, e, j], xdev(e, j))
            s.start()
            tsend[r, d, e, j] = s

    steps = [(r, d) for r in range(R) for d in dorder]
    for r, d in steps[:AHEAD]:
        send_tokens(r, d)

    for r in range(R):
        for d in range(1, Z):
            s = remote(wgt.at[r, c * Y + y], W.at[z, r, y], zs.at[d, r], wr.at[z, y, r], zdev(d))
            s.start()
            pending.append(s)

    def arrived(o, q, r):
        remote(W.at[o, r, q], W.at[o, r, q], zs.at[0, r], wr.at[o, q, r], mate).wait_recv()

    def from_z(r):
        for d in range(1, Z):
            o = lax.rem(z + Z - d, Z)
            arrived(o, y, r)
            for f in range(1, Y):
                s = remote(W.at[o, r, y], W.at[o, r, y], ys.at[f, d, r], wr.at[o, y, r], ydev(f))
                s.start()
                pending.append(s)

    ysend, zsend = {}, {}

    def ypart(q):
        return PT[:, pl.ds(pl.multiple_of(q * L, 128), L)]

    def terms(i, r, d):
        tlocal[r, d].wait()
        for e, j in relations:
            tsend[r, d, e, j].wait_recv()
        if i + AHEAD < len(steps):
            send_tokens(*steps[i + AHEAD])
        total = None
        for b in range(2 * N):
            t = jnp.dot(GT[:, pl.ds(b * B, B)], T[d, pl.ds(b * B, B), pl.ds(r * C, C)], preferred_element_type=F32)
            t = t.astype(BF16).astype(F32)
            total = t if total is None else total + t
        PT[...] = total
        for f in range(1, Y):
            SY[r, d, f - 1] = ypart(yat(f)).astype(BF16)
            s = remote(SY.at[r, d, f - 1], RY.at[r, d, f - 1], sy.at[r, d, f - 1], ry.at[r, d, f - 1], ydev(f))
            s.start()
            ysend[r, d, f] = s
        OWN[r, d] = ypart(y)

    def ysum(r, d):
        total = OWN[r, d]
        for f in range(1, Y):
            ysend[r, d, f].wait_recv()
            total = total + RY[r, d, f - 1].astype(F32)
        if d:
            SZ[r, d - 1] = total.astype(BF16)
            s = remote(SZ.at[r, d - 1], RZ.at[r, d - 1], sz.at[r, d - 1], rz.at[r, d - 1], zdev(d))
            s.start()
            zsend[r, d] = s
        else:
            QF[r] = total

    finals = []
    ysent = {}

    def final(r):
        total = QF[r]
        for d in range(1, Z):
            zsend[r, d].wait_recv()
            total = total + RZ[r, d - 1].astype(F32)
        FIN[r] = total.T
        place = wgrad.at[r, c * Y + y]
        for f in range(1, Y):
            s = remote(FIN.at[r], place, fy.at[r, f - 1], fyr.at[r, f - 1], ydev(f))
            s.start()
            ysent[r, f] = s
        s = remote(FIN.at[r], place, fm.at[r, 0], fmr.at[r, 0], mate)
        s.start()
        finals.append(s)
        a = pltpu.make_async_copy(FIN.at[r], place, fl.at[r])
        a.start()
        locals_.append(a)

    locals_ = []

    def hand_on(r):
        for f in range(1, Y):
            ysent[r, f].wait_recv()
            place = wgrad.at[r, c * Y + lax.rem(y + Y - f, Y)]
            s = remote(place, place, fm.at[r, f], fmr.at[r, f], mate)
            s.start()
            finals.append(s)

    def project(d, first):
        w = W[lax.rem(z + d, Z)].reshape(R * C, M)
        p = jnp.dot(T[d], w, preferred_element_type=F32)
        if first:
            acc[...] = p
        else:
            acc[...] += p

    glocal.wait()
    for e, j in relations:
        gsend[e, j].wait_recv()
    GT[...] = G[...].astype(F32).T.astype(BF16)
    at_step = {}
    for r in range(R):
        at_step.setdefault(min(2 + r, R * Z - 1), []).append(functools.partial(from_z, r))
    for r in range(R - 1):
        at_step.setdefault((r + 1) * Z + min(2, Z - 1), []).append(functools.partial(final, r))
        if r + 2 < R:
            at_step.setdefault((r + 2) * Z, []).append(functools.partial(hand_on, r))
    for i, (r, d) in enumerate(steps):
        terms(i, r, d)
        if i:
            ysum(*steps[i - 1])
        for event in at_step.get(i, []):
            event()
        if i == len(steps) - 1:
            wlocal.wait()
            project(0, True)
    ysum(*steps[-1])
    final(R - 1)
    if R > 1:
        hand_on(R - 2)
    for d in range(1, Z):
        for f in range(1, Y):
            for r in range(R):
                arrived(lax.rem(z + d, Z), yat(f), r)
        project(d, False)
    psend = []
    for i in range(N):
        s = remote(acc.at[block(i, 1 - c), :], PO.at[i], ps.at[i], pr.at[i], mate)
        s.start()
        psend.append(s)
    for s in psend:
        s.wait_recv()
    qsend = []
    for e in range(1, N):
        to = lax.rem(n + e, N)
        XS[e - 1] = acc[block(to, c), :] + PO[to]
        s = remote(XS.at[e - 1], XR.at[e - 1], qs.at[e - 1], qr.at[e - 1], xdev(e, 0))
        s.start()
        qsend.append(s)
    hand_on(R - 1)
    total = acc[mine, :] + PO[n]
    for e in range(1, N):
        qsend[e - 1].wait_recv()
        total = total + XR[e - 1]
    OB[...] = total.astype(BF16)
    olocal = pltpu.make_async_copy(OB, out, ol)
    olocal.start()

    for s in pending + psend + qsend + [s for group in (gsend, tsend, ysend, zsend, ysent) for s in group.values()]:
        s.wait_send()
    for s in finals:
        s.wait()
    for a in locals_:
        a.wait()
    olocal.wait()


def fused(Y, N, Z, tokens, weight, grad_out):
    B, D = tokens.shape
    S, M = weight.shape
    L = 128
    R = S // (2 * Y * L)
    C = Y * L
    DMA = pltpu.SemaphoreType.DMA
    scratch = [
        pltpu.VMEM((Z, 2 * N * B, R * C), BF16),
        pltpu.VMEM((2 * N * B, M), BF16),
        pltpu.VMEM((M, 2 * N * B), BF16),
        pltpu.VMEM((M, C), F32),
        pltpu.VMEM((Z, R, Y, L, M), BF16),
        pltpu.VMEM((R, Z, Y - 1, M, L), BF16),
        pltpu.VMEM((R, Z, Y - 1, M, L), BF16),
        pltpu.VMEM((R, Z, M, L), F32),
        pltpu.VMEM((R, Z - 1, M, L), BF16),
        pltpu.VMEM((R, Z - 1, M, L), BF16),
        pltpu.VMEM((R, M, L), F32),
        pltpu.VMEM((R, L, M), F32),
        pltpu.VMEM((2 * N * B, M), F32),
        pltpu.VMEM((N, B, M), F32),
        pltpu.VMEM((N - 1, B, M), F32),
        pltpu.VMEM((N - 1, B, M), F32),
        pltpu.VMEM((B, M), BF16),
        DMA((R, Z)), DMA((R, Z, N, 2)), DMA((R, Z, N, 2)),
        DMA, DMA((N, 2)), DMA((N, 2)),
        DMA, DMA((Z, Y, R)), DMA((Z, R)), DMA((Y, Z, R)),
        DMA((R, Z, Y - 1)), DMA((R, Z, Y - 1)),
        DMA((R, Z - 1)), DMA((R, Z - 1)),
        DMA((R,)), DMA((R, Y - 1)), DMA((R, Y - 1)), DMA((R, Y)), DMA((R, Y)),
        DMA((N,)), DMA((N,)), DMA((N - 1,)), DMA((N - 1,)), DMA,
    ]
    output, grad = pl.pallas_call(
        functools.partial(kernel, Y, N, Z, R, L, 3),
        out_shape=(jax.ShapeDtypeStruct((B, M), BF16), jax.ShapeDtypeStruct((R, 2 * Y, L, M), F32)),
        in_specs=[pl.BlockSpec(memory_space=pltpu.HBM)] * 3,
        out_specs=(pl.BlockSpec(memory_space=pl.ANY),) * 2,
        scratch_shapes=scratch,
        compiler_params=pltpu.CompilerParams(collective_id=0, has_side_effects=True, vmem_limit_bytes=48 * 2**20),
        cost_estimate=pl.CostEstimate(flops=4 * B * D * M, bytes_accessed=2 * B * D + 6 * S * M, transcendentals=0),
    )(*(pltpu.with_memory_space_constraint(a, pltpu.HBM) for a in (tokens, weight.reshape(R, 2 * Y, L, M), grad_out)))
    return output, grad.reshape(S, M)


def plain(tokens, weight, grad_out):
    model_width = tokens.shape[1]
    out_cols = weight.shape[1]
    projected = jnp.dot(tokens, lax.all_gather(weight, ("node", "gpu"), axis=0, tiled=True), preferred_element_type=F32)
    term = lax.dot_general(tokens, grad_out, (((0,), (0,)), ((), ())), preferred_element_type=F32).astype(BF16)
    stacked = term.reshape(model_width, 1, out_cols)
    received = lax.all_to_all(stacked, ("node", "gpu"), split_axis=0, concat_axis=1, tiled=True)
    own_shard = jnp.sum(received, axis=1, dtype=F32)
    return projected.astype(BF16), lax.psum(own_shard, "group")


def solution(mesh):
    groups, N, Z = (mesh.shape[a] for a in ("group", "node", "gpu"))

    def local(tokens, weight, grad_out):
        if groups % 2 or groups < 4 or N < 2 or Z < 2 or weight.shape[0] % (groups * 128) or tokens.shape[0] % 128:
            return plain(tokens, weight, grad_out)
        return fused(groups // 2, N, Z, tokens, weight, grad_out)

    rows = P(("group", "node", "gpu"), None)
    owners = P(("node", "gpu"), None)
    return jax.shard_map(local, mesh=mesh, in_specs=(rows, owners, rows), out_specs=(rows, owners), check_vma=False)
```

```python
import functools

import jax
import jax.numpy as jnp
from jax import lax
from jax.experimental import pallas as pl
from jax.experimental.pallas import tpu as pltpu
from jax.sharding import PartitionSpec as P

MESH = pl.DeviceIdType.MESH
BF16, F32 = jnp.bfloat16, jnp.float32


def kernel(Y, N, Z, R, L, AHEAD, tok, wgt, gout, out, wgrad, TV, T, G, GT, PT, W, SY, RY, OWN, SZ, RZ, QF, FIN, acc, PO, XS, XR, OB,
           tv, tl, ts, tr, gl, gs, gr, wl, wr, zs, ys, sy, ry, sz, rz, fl, fy, fyr, fm, fmr, ps, pr, qs, qr, ol):
    g, n, z = lax.axis_index("group"), lax.axis_index("node"), lax.axis_index("gpu")
    y, c = g // 2, g % 2
    B = tok.shape[0]
    M = gout.shape[1]
    C = Y * L
    mate = (y * 2 + 1 - c, n, z)
    dorder = list(range(1, Z)) + [0]

    def xdev(e, j):
        core = c if j == 0 else 1 - c
        return (y * 2 + core, lax.rem(n + e, N), z)

    def zdev(d):
        return (g, n, lax.rem(z + d, Z))

    def ydev(f):
        return (lax.rem(y + f, Y) * 2 + c, n, z)

    def yat(f):
        return lax.rem(y + f, Y)

    def remote(src, dst, send, recv, dev):
        return pltpu.make_async_remote_copy(src_ref=src, dst_ref=dst, send_sem=send, recv_sem=recv,
                                            device_id=dev, device_id_type=MESH)

    def block(node, core):
        return pl.ds(pl.multiple_of((node * 2 + core) * B, B), B)

    mine = block(n, c)
    pending = []
    relations = [(e, j) for e in list(range(1, N)) + [0] for j in range(2) if e or j]

    def cols(d, r, e, core):
        o = lax.rem(n + e, N) * Z + lax.rem(z + d, Z)
        return pl.ds(pl.multiple_of(o * (2 * C * R) + r * 2 * C + core * C, 128), C)

    staged = pltpu.make_async_copy(tok, TV, tv)
    staged.start()
    glocal = pltpu.make_async_copy(gout, G.at[mine, :], gl)
    glocal.start()
    tlocal, tsend = {}, {}
    for r in range(R):
        for d in dorder:
            tlocal[r, d] = pltpu.make_async_copy(tok.at[:, cols(d, r, 0, c)], T.at[d, mine, pl.ds(r * C, C)], tl.at[r, d])
            tlocal[r, d].start()
    wlocal = pltpu.make_async_copy(wgt.at[:, pl.ds(c * Y, Y)], W.at[z], wl)
    wlocal.start()

    peers = [xdev(e, j) for e, j in relations] + [zdev(d) for d in range(1, Z)] + [ydev(f) for f in range(1, Y)]
    barrier = pltpu.get_barrier_semaphore()
    for p in peers:
        pl.semaphore_signal(barrier, inc=1, device_id=p, device_id_type=MESH)
    pl.semaphore_wait(barrier, len(peers))

    gsend = {}
    for e, j in relations:
        gsend[e, j] = remote(gout, G.at[mine, :], gs.at[e, j], gr.at[e, j], xdev(e, j))
        gsend[e, j].start()

    def send_tokens(r, d):
        for e, j in relations:
            core = c if j == 0 else 1 - c
            s = remote(TV.at[:, cols(d, r, e, core)], T.at[d, mine, pl.ds(r * C, C)],
                       ts.at[r, d, e, j], tr.at[r, d, e, j], xdev(e, j))
            s.start()
            tsend[r, d, e, j] = s

    steps = [(r, d) for r in range(R) for d in dorder]
    staged.wait()
    for r, d in steps[:AHEAD]:
        send_tokens(r, d)

    for r in range(R):
        for d in range(1, Z):
            s = remote(wgt.at[r, c * Y + y], W.at[z, r, y], zs.at[d, r], wr.at[z, y, r], zdev(d))
            s.start()
            pending.append(s)

    def arrived(o, q, r):
        remote(W.at[o, r, q], W.at[o, r, q], zs.at[0, r], wr.at[o, q, r], mate).wait_recv()

    def from_z(r):
        for d in range(1, Z):
            o = lax.rem(z + Z - d, Z)
            arrived(o, y, r)
            for f in range(1, Y):
                s = remote(W.at[o, r, y], W.at[o, r, y], ys.at[f, d, r], wr.at[o, y, r], ydev(f))
                s.start()
                pending.append(s)

    ysend, zsend = {}, {}

    def ypart(q):
        return PT[:, pl.ds(pl.multiple_of(q * L, 128), L)]

    def terms(i, r, d):
        tlocal[r, d].wait()
        for e, j in relations:
            tsend[r, d, e, j].wait_recv()
        if i + AHEAD < len(steps):
            send_tokens(*steps[i + AHEAD])
        total = None
        for b in range(2 * N):
            t = jnp.dot(GT[:, pl.ds(b * B, B)], T[d, pl.ds(b * B, B), pl.ds(r * C, C)], preferred_element_type=F32)
            t = t.astype(BF16).astype(F32)
            total = t if total is None else total + t
        PT[...] = total
        for f in range(1, Y):
            SY[r, d, f - 1] = ypart(yat(f)).astype(BF16)
            s = remote(SY.at[r, d, f - 1], RY.at[r, d, f - 1], sy.at[r, d, f - 1], ry.at[r, d, f - 1], ydev(f))
            s.start()
            ysend[r, d, f] = s
        OWN[r, d] = ypart(y)

    def ysum(r, d):
        total = OWN[r, d]
        for f in range(1, Y):
            ysend[r, d, f].wait_recv()
            total = total + RY[r, d, f - 1].astype(F32)
        if d:
            SZ[r, d - 1] = total.astype(BF16)
            s = remote(SZ.at[r, d - 1], RZ.at[r, d - 1], sz.at[r, d - 1], rz.at[r, d - 1], zdev(d))
            s.start()
            zsend[r, d] = s
        else:
            QF[r] = total

    finals = []
    ysent = {}

    def final(r):
        total = QF[r]
        for d in range(1, Z):
            zsend[r, d].wait_recv()
            total = total + RZ[r, d - 1].astype(F32)
        FIN[r] = total.T
        place = wgrad.at[r, c * Y + y]
        for f in range(1, Y):
            s = remote(FIN.at[r], place, fy.at[r, f - 1], fyr.at[r, f - 1], ydev(f))
            s.start()
            ysent[r, f] = s
        s = remote(FIN.at[r], place, fm.at[r, 0], fmr.at[r, 0], mate)
        s.start()
        finals.append(s)
        a = pltpu.make_async_copy(FIN.at[r], place, fl.at[r])
        a.start()
        locals_.append(a)

    locals_ = []

    def hand_on(r):
        for f in range(1, Y):
            ysent[r, f].wait_recv()
            place = wgrad.at[r, c * Y + lax.rem(y + Y - f, Y)]
            s = remote(place, place, fm.at[r, f], fmr.at[r, f], mate)
            s.start()
            finals.append(s)

    def project(d, first):
        w = W[lax.rem(z + d, Z)].reshape(R * C, M)
        p = jnp.dot(T[d], w, preferred_element_type=F32)
        if first:
            acc[...] = p
        else:
            acc[...] += p

    glocal.wait()
    for e, j in relations:
        gsend[e, j].wait_recv()
    GT[...] = G[...].astype(F32).T.astype(BF16)
    at_step = {}
    for r in range(R):
        at_step.setdefault(min(2 + r, R * Z - 1), []).append(functools.partial(from_z, r))
    for r in range(R - 1):
        at_step.setdefault((r + 1) * Z + min(2, Z - 1), []).append(functools.partial(final, r))
        if r + 2 < R:
            at_step.setdefault((r + 2) * Z, []).append(functools.partial(hand_on, r))
    for i, (r, d) in enumerate(steps):
        terms(i, r, d)
        if i:
            ysum(*steps[i - 1])
        for event in at_step.get(i, []):
            event()
        if i == len(steps) - 1:
            wlocal.wait()
            project(0, True)
    ysum(*steps[-1])
    final(R - 1)
    if R > 1:
        hand_on(R - 2)
    for d in range(1, Z):
        for f in range(1, Y):
            for r in range(R):
                arrived(lax.rem(z + d, Z), yat(f), r)
        project(d, False)
    psend = []
    for i in range(N):
        s = remote(acc.at[block(i, 1 - c), :], PO.at[i], ps.at[i], pr.at[i], mate)
        s.start()
        psend.append(s)
    for s in psend:
        s.wait_recv()
    qsend = []
    for e in range(1, N):
        to = lax.rem(n + e, N)
        XS[e - 1] = acc[block(to, c), :] + PO[to]
        s = remote(XS.at[e - 1], XR.at[e - 1], qs.at[e - 1], qr.at[e - 1], xdev(e, 0))
        s.start()
        qsend.append(s)
    hand_on(R - 1)
    total = acc[mine, :] + PO[n]
    for e in range(1, N):
        qsend[e - 1].wait_recv()
        total = total + XR[e - 1]
    OB[...] = total.astype(BF16)
    olocal = pltpu.make_async_copy(OB, out, ol)
    olocal.start()

    for s in pending + psend + qsend + [s for group in (gsend, tsend, ysend, zsend, ysent) for s in group.values()]:
        s.wait_send()
    for s in finals:
        s.wait()
    for a in locals_:
        a.wait()
    olocal.wait()


def fused(Y, N, Z, tokens, weight, grad_out):
    B, D = tokens.shape
    S, M = weight.shape
    L = 128
    R = S // (2 * Y * L)
    C = Y * L
    DMA = pltpu.SemaphoreType.DMA
    scratch = [
        pltpu.VMEM((B, D), BF16),
        pltpu.VMEM((Z, 2 * N * B, R * C), BF16),
        pltpu.VMEM((2 * N * B, M), BF16),
        pltpu.VMEM((M, 2 * N * B), BF16),
        pltpu.VMEM((M, C), F32),
        pltpu.VMEM((Z, R, Y, L, M), BF16),
        pltpu.VMEM((R, Z, Y - 1, M, L), BF16),
        pltpu.VMEM((R, Z, Y - 1, M, L), BF16),
        pltpu.VMEM((R, Z, M, L), F32),
        pltpu.VMEM((R, Z - 1, M, L), BF16),
        pltpu.VMEM((R, Z - 1, M, L), BF16),
        pltpu.VMEM((R, M, L), F32),
        pltpu.VMEM((R, L, M), F32),
        pltpu.VMEM((2 * N * B, M), F32),
        pltpu.VMEM((N, B, M), F32),
        pltpu.VMEM((N - 1, B, M), F32),
        pltpu.VMEM((N - 1, B, M), F32),
        pltpu.VMEM((B, M), BF16),
        DMA, DMA((R, Z)), DMA((R, Z, N, 2)), DMA((R, Z, N, 2)),
        DMA, DMA((N, 2)), DMA((N, 2)),
        DMA, DMA((Z, Y, R)), DMA((Z, R)), DMA((Y, Z, R)),
        DMA((R, Z, Y - 1)), DMA((R, Z, Y - 1)),
        DMA((R, Z - 1)), DMA((R, Z - 1)),
        DMA((R,)), DMA((R, Y - 1)), DMA((R, Y - 1)), DMA((R, Y)), DMA((R, Y)),
        DMA((N,)), DMA((N,)), DMA((N - 1,)), DMA((N - 1,)), DMA,
    ]
    output, grad = pl.pallas_call(
        functools.partial(kernel, Y, N, Z, R, L, 2),
        out_shape=(jax.ShapeDtypeStruct((B, M), BF16), jax.ShapeDtypeStruct((R, 2 * Y, L, M), F32)),
        in_specs=[pl.BlockSpec(memory_space=pltpu.HBM)] * 3,
        out_specs=(pl.BlockSpec(memory_space=pl.ANY),) * 2,
        scratch_shapes=scratch,
        compiler_params=pltpu.CompilerParams(collective_id=0, has_side_effects=True, vmem_limit_bytes=48 * 2**20),
        cost_estimate=pl.CostEstimate(flops=4 * B * D * M, bytes_accessed=2 * B * D + 6 * S * M, transcendentals=0),
    )(*(pltpu.with_memory_space_constraint(a, pltpu.HBM) for a in (tokens, weight.reshape(R, 2 * Y, L, M), grad_out)))
    return output, grad.reshape(S, M)


def plain(tokens, weight, grad_out):
    model_width = tokens.shape[1]
    out_cols = weight.shape[1]
    projected = jnp.dot(tokens, lax.all_gather(weight, ("node", "gpu"), axis=0, tiled=True), preferred_element_type=F32)
    term = lax.dot_general(tokens, grad_out, (((0,), (0,)), ((), ())), preferred_element_type=F32).astype(BF16)
    stacked = term.reshape(model_width, 1, out_cols)
    received = lax.all_to_all(stacked, ("node", "gpu"), split_axis=0, concat_axis=1, tiled=True)
    own_shard = jnp.sum(received, axis=1, dtype=F32)
    return projected.astype(BF16), lax.psum(own_shard, "group")


def solution(mesh):
    groups, N, Z = (mesh.shape[a] for a in ("group", "node", "gpu"))

    def local(tokens, weight, grad_out):
        if groups % 2 or groups < 4 or N < 2 or Z < 2 or weight.shape[0] % (groups * 128) or tokens.shape[0] % 128:
            return plain(tokens, weight, grad_out)
        return fused(groups // 2, N, Z, tokens, weight, grad_out)

    rows = P(("group", "node", "gpu"), None)
    owners = P(("node", "gpu"), None)
    return jax.shard_map(local, mesh=mesh, in_specs=(rows, owners, rows), out_specs=(rows, owners), check_vma=False)
```

```python
import functools

import jax
import jax.numpy as jnp
from jax import lax
from jax.experimental import pallas as pl
from jax.experimental.pallas import tpu as pltpu
from jax.sharding import PartitionSpec as P

MESH = pl.DeviceIdType.MESH
BF16, F32 = jnp.bfloat16, jnp.float32


def kernel(Y, N, Z, R, L, AHEAD, tok, wgt, gout, out, wgrad, T, G, GT, PT, W, SY, RY, OWN, SZ, RZ, QF, FIN, acc, PO, XS, XR, OB,
           tl, ts, tr, gl, gs, gr, wl, wr, zs, ys, sy, ry, sz, rz, fl, fy, fyr, fm, fmr, ps, pr, qs, qr, ol):
    g, n, z = lax.axis_index("group"), lax.axis_index("node"), lax.axis_index("gpu")
    y, c = g // 2, g % 2
    B = tok.shape[0]
    M = gout.shape[1]
    C = Y * L
    mate = (y * 2 + 1 - c, n, z)
    dorder = list(range(1, Z)) + [0]

    def xdev(e, j):
        core = c if j == 0 else 1 - c
        return (y * 2 + core, lax.rem(n + e, N), z)

    def zdev(d):
        return (g, n, lax.rem(z + d, Z))

    def ydev(f):
        return (lax.rem(y + f, Y) * 2 + c, n, z)

    def yat(f):
        return lax.rem(y + f, Y)

    def remote(src, dst, send, recv, dev):
        return pltpu.make_async_remote_copy(src_ref=src, dst_ref=dst, send_sem=send, recv_sem=recv,
                                            device_id=dev, device_id_type=MESH)

    def block(node, core):
        return pl.ds(pl.multiple_of((node * 2 + core) * B, B), B)

    mine = block(n, c)
    pending = []
    relations = [(e, j) for e in list(range(1, N)) + [0] for j in range(2) if e or j]

    def cols(d, r, e, core):
        o = lax.rem(n + e, N) * Z + lax.rem(z + d, Z)
        return pl.ds(pl.multiple_of(o * (2 * C * R) + r * 2 * C + core * C, 128), C)

    glocal = pltpu.make_async_copy(gout, G.at[mine, :], gl)
    glocal.start()
    tlocal, tsend = {}, {}
    for r in range(R):
        for d in dorder:
            tlocal[r, d] = pltpu.make_async_copy(tok.at[:, cols(d, r, 0, c)], T.at[d, mine, pl.ds(r * C, C)], tl.at[r, d])
            tlocal[r, d].start()
    wlocal = pltpu.make_async_copy(wgt.at[:, pl.ds(c * Y, Y)], W.at[z], wl)
    wlocal.start()

    peers = [xdev(e, j) for e, j in relations] + [zdev(d) for d in range(1, Z)] + [ydev(f) for f in range(1, Y)]
    barrier = pltpu.get_barrier_semaphore()
    for p in peers:
        pl.semaphore_signal(barrier, inc=1, device_id=p, device_id_type=MESH)
    pl.semaphore_wait(barrier, len(peers))

    gsend = {}
    for e, j in relations:
        if e == 0 or j == 0:
            gsend[e, j] = remote(gout, G.at[mine, :], gs.at[e, j], gr.at[e, j], xdev(e, j))
            gsend[e, j].start()

    def send_tokens(r, d):
        for e, j in relations:
            core = c if j == 0 else 1 - c
            s = remote(tok.at[:, cols(d, r, e, core)], T.at[d, mine, pl.ds(r * C, C)],
                       ts.at[r, d, e, j], tr.at[r, d, e, j], xdev(e, j))
            s.start()
            tsend[r, d, e, j] = s

    steps = [(r, d) for r in range(R) for d in dorder]
    for r, d in steps[:AHEAD]:
        send_tokens(r, d)

    for d in range(1, Z):
        s = remote(wgt.at[:, c * Y + y], W.at[z, :, y], zs.at[d], wr.at[z, y], zdev(d))
        s.start()
        pending.append(s)

    def arrived(o, q):
        remote(W.at[o, :, q], W.at[o, :, q], zs.at[0], wr.at[o, q], mate).wait_recv()

    def from_z(d):
        o = lax.rem(z + Z - d, Z)
        arrived(o, y)
        for f in range(1, Y):
            s = remote(W.at[o, :, y], W.at[o, :, y], ys.at[f, d], wr.at[o, y], ydev(f))
            s.start()
            pending.append(s)

    ysend, zsend = {}, {}

    def ypart(q):
        return PT[:, pl.ds(pl.multiple_of(q * L, 128), L)]

    def terms(i, r, d):
        tlocal[r, d].wait()
        for e, j in relations:
            tsend[r, d, e, j].wait_recv()
        if i + AHEAD < len(steps):
            send_tokens(*steps[i + AHEAD])
        total = None
        for b in range(2 * N):
            t = jnp.dot(GT[:, pl.ds(b * B, B)], T[d, pl.ds(b * B, B), pl.ds(r * C, C)], preferred_element_type=F32)
            t = t.astype(BF16).astype(F32)
            total = t if total is None else total + t
        PT[...] = total
        for f in range(1, Y):
            SY[r, d, f - 1] = ypart(yat(f)).astype(BF16)
            s = remote(SY.at[r, d, f - 1], RY.at[r, d, f - 1], sy.at[r, d, f - 1], ry.at[r, d, f - 1], ydev(f))
            s.start()
            ysend[r, d, f] = s
        OWN[r, d] = ypart(y)

    def ysum(r, d):
        total = OWN[r, d]
        for f in range(1, Y):
            ysend[r, d, f].wait_recv()
            total = total + RY[r, d, f - 1].astype(F32)
        if d:
            SZ[r, d - 1] = total.astype(BF16)
            s = remote(SZ.at[r, d - 1], RZ.at[r, d - 1], sz.at[r, d - 1], rz.at[r, d - 1], zdev(d))
            s.start()
            zsend[r, d] = s
        else:
            QF[r] = total

    finals = []
    ysent = {}

    def final(r):
        total = QF[r]
        for d in range(1, Z):
            zsend[r, d].wait_recv()
            total = total + RZ[r, d - 1].astype(F32)
        FIN[r] = total.T
        place = wgrad.at[r, c * Y + y]
        for f in range(1, Y):
            s = remote(FIN.at[r], place, fy.at[r, f - 1], fyr.at[r, f - 1], ydev(f))
            s.start()
            ysent[r, f] = s
        s = remote(FIN.at[r], place, fm.at[r, 0], fmr.at[r, 0], mate)
        s.start()
        finals.append(s)
        a = pltpu.make_async_copy(FIN.at[r], place, fl.at[r])
        a.start()
        locals_.append(a)

    locals_ = []

    def hand_on(r):
        for f in range(1, Y):
            ysent[r, f].wait_recv()
            place = wgrad.at[r, c * Y + lax.rem(y + Y - f, Y)]
            s = remote(place, place, fm.at[r, f], fmr.at[r, f], mate)
            s.start()
            finals.append(s)

    def project(d, lo, hi, first):
        o = lax.rem(z + d, Z)
        w = W[o, lo:hi].reshape((hi - lo) * C, M)
        p = jnp.dot(T[d, :, lo * C:hi * C], w, preferred_element_type=F32)
        if first:
            acc[...] = p
        else:
            acc[...] += p

    def weights(d):
        if d:
            for f in range(1, Y):
                arrived(lax.rem(z + d, Z), yat(f))
        else:
            wlocal.wait()

    glocal.wait()
    for e in range(1, N):
        gsend[e, 0].wait_recv()
        rows = G.at[block(lax.rem(n + N - e, N), c), :]
        gsend[e, 1] = remote(rows, rows, gs.at[e, 1], gr.at[e, 1], mate)
        gsend[e, 1].start()
    gsend[0, 1].wait_recv()
    for e in range(1, N):
        gsend[e, 1].wait_recv()
    GT[...] = G[...].astype(F32).T.astype(BF16)
    at_step = {}
    for i, d in enumerate(range(1, Z)):
        at_step.setdefault(min(Z - 1 + i, (R - 1) * Z - 1), []).append(functools.partial(from_z, d))
    for r in range(R - 1):
        at_step.setdefault((r + 1) * Z + min(2, Z - 1), []).append(functools.partial(final, r))
        if r + 2 < R:
            at_step.setdefault((r + 2) * Z, []).append(functools.partial(hand_on, r))
    for i, (r, d) in enumerate(steps):
        terms(i, r, d)
        if i:
            ysum(*steps[i - 1])
        for event in at_step.get(i, []):
            event()
        if r == R - 1:
            weights(d)
            if R > 1:
                project(d, 0, R - 1, d == dorder[0])
    ysum(*steps[-1])
    for d in dorder:
        project(d, R - 1, R, R == 1 and d == dorder[0])
    psend = []
    for i in range(N):
        s = remote(acc.at[block(i, 1 - c), :], PO.at[i], ps.at[i], pr.at[i], mate)
        s.start()
        psend.append(s)
    for s in psend:
        s.wait_recv()
    qsend = []
    for e in range(1, N):
        to = lax.rem(n + e, N)
        XS[e - 1] = acc[block(to, c), :] + PO[to]
        s = remote(XS.at[e - 1], XR.at[e - 1], qs.at[e - 1], qr.at[e - 1], xdev(e, 0))
        s.start()
        qsend.append(s)
    final(R - 1)
    if R > 1:
        hand_on(R - 2)
    total = acc[mine, :] + PO[n]
    for e in range(1, N):
        qsend[e - 1].wait_recv()
        total = total + XR[e - 1]
    OB[...] = total.astype(BF16)
    olocal = pltpu.make_async_copy(OB, out, ol)
    olocal.start()
    hand_on(R - 1)

    for s in pending + psend + qsend + [s for group in (gsend, tsend, ysend, zsend, ysent) for s in group.values()]:
        s.wait_send()
    for s in finals:
        s.wait()
    for a in locals_:
        a.wait()
    olocal.wait()


def fused(Y, N, Z, tokens, weight, grad_out):
    B, D = tokens.shape
    S, M = weight.shape
    L = 128
    R = S // (2 * Y * L)
    C = Y * L
    DMA = pltpu.SemaphoreType.DMA
    scratch = [
        pltpu.VMEM((Z, 2 * N * B, R * C), BF16),
        pltpu.VMEM((2 * N * B, M), BF16),
        pltpu.VMEM((M, 2 * N * B), BF16),
        pltpu.VMEM((M, C), F32),
        pltpu.VMEM((Z, R, Y, L, M), BF16),
        pltpu.VMEM((R, Z, Y - 1, M, L), BF16),
        pltpu.VMEM((R, Z, Y - 1, M, L), BF16),
        pltpu.VMEM((R, Z, M, L), F32),
        pltpu.VMEM((R, Z - 1, M, L), BF16),
        pltpu.VMEM((R, Z - 1, M, L), BF16),
        pltpu.VMEM((R, M, L), F32),
        pltpu.VMEM((R, L, M), F32),
        pltpu.VMEM((2 * N * B, M), F32),
        pltpu.VMEM((N, B, M), F32),
        pltpu.VMEM((N - 1, B, M), F32),
        pltpu.VMEM((N - 1, B, M), F32),
        pltpu.VMEM((B, M), BF16),
        DMA((R, Z)), DMA((R, Z, N, 2)), DMA((R, Z, N, 2)),
        DMA, DMA((N, 2)), DMA((N, 2)),
        DMA, DMA((Z, Y)), DMA((Z,)), DMA((Y, Z)),
        DMA((R, Z, Y - 1)), DMA((R, Z, Y - 1)),
        DMA((R, Z - 1)), DMA((R, Z - 1)),
        DMA((R,)), DMA((R, Y - 1)), DMA((R, Y - 1)), DMA((R, Y)), DMA((R, Y)),
        DMA((N,)), DMA((N,)), DMA((N - 1,)), DMA((N - 1,)), DMA,
    ]
    output, grad = pl.pallas_call(
        functools.partial(kernel, Y, N, Z, R, L, 2),
        out_shape=(jax.ShapeDtypeStruct((B, M), BF16), jax.ShapeDtypeStruct((R, 2 * Y, L, M), F32)),
        in_specs=[pl.BlockSpec(memory_space=pltpu.HBM)] * 3,
        out_specs=(pl.BlockSpec(memory_space=pl.ANY),) * 2,
        scratch_shapes=scratch,
        compiler_params=pltpu.CompilerParams(collective_id=0, has_side_effects=True, vmem_limit_bytes=48 * 2**20),
        cost_estimate=pl.CostEstimate(flops=4 * B * D * M, bytes_accessed=2 * B * D + 6 * S * M, transcendentals=0),
    )(*(pltpu.with_memory_space_constraint(a, pltpu.HBM) for a in (tokens, weight.reshape(R, 2 * Y, L, M), grad_out)))
    return output, grad.reshape(S, M)


def plain(tokens, weight, grad_out):
    model_width = tokens.shape[1]
    out_cols = weight.shape[1]
    projected = jnp.dot(tokens, lax.all_gather(weight, ("node", "gpu"), axis=0, tiled=True), preferred_element_type=F32)
    term = lax.dot_general(tokens, grad_out, (((0,), (0,)), ((), ())), preferred_element_type=F32).astype(BF16)
    stacked = term.reshape(model_width, 1, out_cols)
    received = lax.all_to_all(stacked, ("node", "gpu"), split_axis=0, concat_axis=1, tiled=True)
    own_shard = jnp.sum(received, axis=1, dtype=F32)
    return projected.astype(BF16), lax.psum(own_shard, "group")


def solution(mesh):
    groups, N, Z = (mesh.shape[a] for a in ("group", "node", "gpu"))

    def local(tokens, weight, grad_out):
        if groups % 2 or groups < 4 or N < 2 or Z < 2 or weight.shape[0] % (groups * 128) or tokens.shape[0] % 128:
            return plain(tokens, weight, grad_out)
        return fused(groups // 2, N, Z, tokens, weight, grad_out)

    rows = P(("group", "node", "gpu"), None)
    owners = P(("node", "gpu"), None)
    return jax.shard_map(local, mesh=mesh, in_specs=(rows, owners, rows), out_specs=(rows, owners), check_vma=False)
```
